128 devices in a mesh: sp: 32 (over x, z, y_hi), ch: 4 (over y_lo, core).
Axes of the slice: x: 4, y: 4 (y_hi: 2, y_lo: 2; y = y_hi * 2 + y_lo), z: 4, core: 2. Of those that a mesh axis runs over, the one named last changes fastest.
Arguments:
- features: bfloat16 [64, 256, 1024], P('sp', 'ch'), may hold values from -6 to 6
- weight: bfloat16 [27, 256, 256], P(None, 'ch'), may hold values from -0.078125 to 0.078125
- cotangent: bfloat16 [64, 256, 1024], P('sp', 'ch'), may hold values from -6 to 6
Outputs:
- grad_input: float32 [64, 256, 1024], P('sp', 'ch')
- grad_weight: float32 [27, 256, 256], P(None, 'ch')
The draws below stay inside these ranges and needn't reach their ends.
All inputs are finite; a program needn't handle non-finite values.
Results may differ from the reference program's by a relative error of at most 0.0029.
Values may be sent and summed in bfloat16 or wider, within the bound.
A program may use at most 128 MiB of HBM per device.

```python
import math
import jax
import jax.numpy as jnp
from jax import lax

C_IN = 256
C_OUT = 256
HEIGHT = 32
WIDTH = 32
DEPTH = 64
CELLS = 65536


def block_scale(key, shape, split, smallest, high):
    def one(dim, shards_of):
        steps = jax.random.uniform(jax.random.fold_in(jax.random.fold_in(key, 6), dim), (shards_of,), jnp.float32, smallest / len(split), high / len(split))
        return jnp.repeat(jnp.exp(steps), shape[dim] // shards_of).reshape((-1,) + (1,) * (len(shape) - dim - 1))

    gain = one(*split[0])
    for cut in split[1:]:
        gain = gain * one(*cut)
    return gain


def noise(own_key, dims, scale, bound, cuts=(), dtype=jnp.bfloat16):
    values = jax.random.normal(own_key, dims, jnp.float32) * scale
    if len(cuts) > 0:
        values = block_scale(own_key, dims, cuts, -0.22, 0.18) * values
    return jnp.clip(values, min=-bound, max=bound).astype(dtype)


def setup_inputs(seed: int = 0) -> dict:
    streams_of = jax.random.split(jax.random.key(seed), 4)
    features = noise(streams_of[0], (DEPTH, C_IN, HEIGHT * WIDTH), 1.0, 6.0, ((0, 32), (1, 4)))
    weight = noise(streams_of[1], (27, C_OUT, C_IN), (27 * C_IN) ** -0.5, 0.078125, ((1, 4),))
    cotangent = noise(streams_of[2], (DEPTH, C_OUT, HEIGHT * WIDTH), 1.0, 6.0, ((0, 32), (1, 4)))
    return {"features": features, "weight": weight, "cotangent": cotangent}


def spread(field):
    planes, chans, _ = field.shape
    grid = field.reshape(planes, chans, HEIGHT, WIDTH)
    return jnp.pad(grid, ((1, 1), (0, 0), (1, 1), (1, 1)))

def window(padded, shift_d, shift_h, shift_w, planes):
    piece = padded[shift_d:shift_d + planes, :, shift_h:shift_h + HEIGHT, shift_w:shift_w + WIDTH]
    return piece.reshape(planes, padded.shape[1], HEIGHT * WIDTH).astype(jnp.float32)

def reference(features, weight, cotangent):
    planes = features.shape[0]
    outputs = weight.shape[1]
    best = lax.Precision.HIGHEST
    padded = spread(features)
    wide_weight = weight.astype(jnp.float32)
    preact = jnp.zeros((planes, outputs, HEIGHT * WIDTH), jnp.float32)
    for stencil in range(27):
        patch = window(padded, stencil // 9, stencil // 3 % 3, stencil % 3, planes)
        preact = preact + jnp.einsum('dcp,oc->dop', patch, wide_weight[stencil], precision=best)
    sigmoid_pre = jax.nn.sigmoid(preact)
    slope = sigmoid_pre * (1.0 + preact * (1.0 - sigmoid_pre))
    grad_pre = (cotangent.astype(jnp.float32) * slope).astype(jnp.bfloat16)
    wide_grad = grad_pre.astype(jnp.float32)
    partial_grads = []
    for stencil in range(27):
        patch = window(padded, stencil // 9, stencil // 3 % 3, stencil % 3, planes)
        partial_grads.append(jnp.einsum('dcp,dop->oc', patch, wide_grad, precision=best))
    grad_weight = jnp.stack(partial_grads) / math.sqrt(CELLS)
    grad_pad = spread(grad_pre)
    summed = jnp.zeros(features.shape, jnp.float32)
    for stencil in range(27):
        moved = window(grad_pad, 2 - stencil // 9, 2 - stencil // 3 % 3, 2 - stencil % 3, planes)
        summed = summed + jnp.einsum('dop,oc->dcp', moved, wide_weight[stencil], precision=best)
    return (summed, grad_weight)
```

```python
import functools

import jax
import jax.numpy as jnp
from jax import lax
from jax.experimental import pallas as pl
from jax.experimental.pallas import tpu as pltpu
from jax.sharding import PartitionSpec as P

MESH = pl.DeviceIdType.MESH
F32, BF16 = jnp.float32, jnp.bfloat16
WIDTH = 32
CELLS = 1024
QUARTER = 64
FULL = 256
STACK = 9 * QUARTER
TILE = 256
STRIDE = 640
IN_TILE, OUT_TILE, D_TILE, ROWS = 256, 256, 256, 64
ROLL = BF16
CHUNKS = ((0, 8, 2), (8, 8, 2), (16, 11, 3))
SLOTS = 28
SCALE = 1.0 / 256.0


def wrap(value, size):
    return lax.rem(value, size)


def place():
    sp, ch = lax.axis_index("sp"), lax.axis_index("ch")
    return sp, ch, lax.div(sp, 8), lax.rem(lax.div(sp, 2), 4), lax.rem(sp, 2)


def index(x, z, y):
    return x * 8 + z * 2 + y


def roll(value, shift):
    return pltpu.roll(value, shift % CELLS, 1)


def nine(value, lane, column):
    zero = jnp.zeros_like(value)
    wide = [
        jnp.where(column <= WIDTH - 2, roll(value, -1), zero),
        value,
        jnp.where(column >= 1, roll(value, 1), zero),
    ]
    out = [jnp.where(lane < CELLS - WIDTH, roll(v, -WIDTH), zero) for v in wide]
    out += wide
    out += [jnp.where(lane >= WIDTH, roll(v, WIDTH), zero) for v in wide]
    return out


def lanes(rows):
    lane = lax.broadcasted_iota(jnp.int32, (rows, CELLS), 1)
    return lane, lax.rem(lane, WIDTH)


def shift_in(value, row, rows, stacked, plane):
    lane, column = lanes(rows)
    for s, moved in enumerate(nine(value, lane, column)):
        stacked[pl.ds(plane * STRIDE + s * QUARTER + row, rows), :] = moved.astype(BF16)


def kernel(
    f_ref, cot_ref, w_ref, gi_ref, out_ref,
    planes, edge, cot, wide_in, wide_out, turned_in, turned_out, taps_out, stacked, gedge, ghalo,
    part, exact, sum_x, sum_z, got1, got2, middle, got3, dx, dsend, dgot, dsend2, dgot2,
    local_sem, send_sem, recv_sem,
):
    sp, ch, x, z, y = place()
    other = wrap(ch + 2, 4)
    twin = lax.div(ch, 2) * 2 + wrap(ch + 1, 2)
    twin_other = wrap(twin + 2, 4)
    up, down = wrap(sp + 1, 32), wrap(sp + 31, 32)

    def near(dx_, dz_, dy_):
        return index(wrap(x + dx_, 4), wrap(z + dz_, 4), wrap(y + dy_, 2))

    barrier = pltpu.get_barrier_semaphore()
    friends = [(sp, twin), (sp, other), (up, ch), (down, ch), (up, other), (down, other)]
    friends += [(near(d, 0, 0), ch) for d in (1, 2, 3)] + [(near(0, d, 0), ch) for d in (1, 2, 3)]
    friends.append((near(0, 0, 1), ch))
    for friend in friends:
        pl.semaphore_signal(barrier, inc=1, device_id=friend, device_id_type=MESH)

    own = pl.ds(1, 2)
    mine = pl.ds(pl.multiple_of(ch * QUARTER, QUARTER), QUARTER)
    others = pl.ds(pl.multiple_of(other * QUARTER, QUARTER), QUARTER)
    twins = pl.ds(pl.multiple_of(twin * QUARTER, QUARTER), QUARTER)
    twin_others = pl.ds(pl.multiple_of(twin_other * QUARTER, QUARTER), QUARTER)

    loads = [(f_ref, planes.at[own, mine])]
    low, high = pl.ds(0, STACK), pl.ds(STACK, STACK)
    left, right = pl.ds(0, FULL), pl.ds(FULL, FULL)
    loads += [(w_ref.at[1], wide_in.at[low, left]), (w_ref.at[2], wide_in.at[low, right])]
    loads += [(w_ref.at[0], wide_in.at[high, left]), (w_ref.at[1], wide_in.at[high, right])]
    loads += [(w_ref.at[0], wide_out.at[0]), (w_ref.at[2], wide_out.at[1]), (cot_ref, cot)]
    loads = [pltpu.make_async_copy(src, dst, local_sem.at[i]) for i, (src, dst) in enumerate(loads)]
    for load in loads:
        load.start()
    loads[0].wait()
    for e, plane, inside in ((0, 2, sp < 31), (1, 1, sp > 0)):
        value = planes[plane, mine, :]
        edge[e] = jnp.where(inside, value, jnp.zeros_like(value))
    pl.semaphore_wait(barrier, len(friends))

    sent = []

    def go(src, dst, device, lands):
        i = len(sent)

        def copy_to(ref):
            return pltpu.make_async_remote_copy(
                src_ref=src, dst_ref=ref, send_sem=send_sem.at[i], recv_sem=recv_sem.at[i],
                device_id=device, device_id_type=MESH,
            )

        copy = copy_to(dst)
        copy.start()
        sent.append(copy)
        return copy_to(lands)

    mine_own = planes.at[own, mine]
    across = go(mine_own, mine_own, (sp, other), planes.at[own, others])
    beside = go(mine_own, mine_own, (sp, twin), planes.at[own, twins])

    def halos(core, rows):
        out = []
        for e, peer, slot in ((0, up, 0), (1, down, 3)):
            out.append((slot, go(edge.at[e], planes.at[slot, mine], (peer, core), planes.at[slot, rows])))
        return out

    def passing(landings, rows, arriving):
        out = []
        for slot, landing in landings:
            landing.wait_recv()
            out.append(go(planes.at[slot, rows], planes.at[slot, rows], (sp, twin), planes.at[slot, arriving]))
        return out

    halo_mine = halos(ch, mine)
    halo_other = halos(other, others)

    for load in loads[1:]:
        load.wait()
    for p in range(4):
        stacked[pl.ds(p * STRIDE + STACK, STRIDE - STACK), :] = jnp.zeros((STRIDE - STACK, CELLS), BF16)
    pad = jnp.zeros((FULL, STRIDE - STACK), BF16)
    for a, src, places in (
        (0, wide_out.at[0], (turned_in.at[0, :, pl.ds(STRIDE, STRIDE)], turned_out.at[1])),
        (1, wide_in.at[low, left], (turned_in.at[0, :, pl.ds(0, STRIDE)], turned_in.at[1, :, pl.ds(STRIDE, STRIDE)])),
        (2, wide_out.at[1], (turned_in.at[1, :, pl.ds(0, STRIDE)], turned_out.at[0])),
    ):
        for k in range(0, STACK, 128):
            n = min(128, STACK - k)
            block = src[pl.ds(k, n), :].T
            for dst in places:
                dst[:, pl.ds(k, n)] = block
        for dst in places:
            dst[:, pl.ds(STACK, STRIDE - STACK)] = pad

    across.wait_recv()
    passed = go(planes.at[own, others], planes.at[own, others], (sp, twin), planes.at[own, twin_others])
    passes = passing(halo_other, others, twin_others)
    beside.wait_recv()
    passed.wait_recv()

    for n in range(0, CELLS, IN_TILE):
        cols = pl.ds(n, IN_TILE)
        taps_out[:, cols] = jnp.dot(
            wide_in[...], planes[own, :, cols].reshape(2 * FULL, IN_TILE), preferred_element_type=F32
        )

    passes += passing(halo_mine, mine, twins)
    for landing in passes:
        landing.wait_recv()

    def outer(d):
        for n in range(0, CELLS, OUT_TILE):
            cols = pl.ds(n, OUT_TILE)
            taps_out[pl.ds(d * STACK, STACK), cols] += jnp.dot(
                wide_out[d], planes[3 * d, :, cols], preferred_element_type=F32
            )

    rows = ROWS

    def slope(d, inside):
        def body(o, carry):
            at = pl.multiple_of(o * rows, rows)
            lane, column = lanes(rows)

            def tap(b, c):
                return taps_out[pl.ds(d * STACK + (3 * b + c) * QUARTER + at, rows), :]

            pre = None
            for c in range(3):
                total = tap(1, c)
                total = total + jnp.where(lane >= WIDTH, roll(tap(0, c), WIDTH), 0.0)
                total = total + jnp.where(lane < CELLS - WIDTH, roll(tap(2, c), -WIDTH), 0.0)
                if c == 0:
                    total = jnp.where(column >= 1, roll(total, 1), 0.0)
                if c == 2:
                    total = jnp.where(column <= WIDTH - 2, roll(total, -1), 0.0)
                pre = total if pre is None else pre + total
            s = 1.0 / (1.0 + jnp.exp(-pre))
            grad = cot[d, pl.ds(at, rows), :].astype(F32) * (s * (1.0 + pre * (1.0 - s)))
            grad = grad.astype(BF16)
            gedge[d, pl.ds(at, rows), :] = jnp.where(inside, grad, jnp.zeros_like(grad))
            shift_in(grad.astype(ROLL), at, rows, stacked, 1 + d)
            return carry

        lax.fori_loop(0, QUARTER // rows, body, 0)

    outer(0)
    slope(0, sp > 0)
    g_down = go(gedge.at[0], ghalo.at[1], (down, ch), ghalo.at[1])
    outer(1)
    slope(1, sp < 31)
    g_up = go(gedge.at[1], ghalo.at[0], (up, ch), ghalo.at[0])

    contract = (((1,), (1,)), ((), ()))

    def wgrad(a):
        total = None
        for d in range(2):
            term = lax.dot_general(
                stacked[pl.ds((1 + d) * STRIDE, STACK), :], planes[a + d], contract,
                preferred_element_type=F32,
            )
            total = term if total is None else total + term
        exact[pl.ds(a * 9, 9)] = total.reshape(9, QUARTER, FULL)
        part[pl.ds(a * 9, 9)] = total.astype(BF16).reshape(9, QUARTER, FULL)

    line_x = [(near(d, 0, 0), wrap(x + d, 4), wrap(x + 4 - d, 4)) for d in (1, 2, 3)]
    line_z = [(near(0, d, 0), wrap(z + d, 4), wrap(z + 4 - d, 4)) for d in (1, 2, 3)]
    halves = (
        dict(slot=0, cols=pl.ds(0, 128), me=x, line=line_x, owner=z, group=line_z, total=sum_x),
        dict(slot=1, cols=pl.ds(128, 128), me=z, line=line_z, owner=x, group=line_x, total=sum_z),
    )
    mate = (near(0, 0, 1), ch)

    def tile16(i):
        return pl.ds(pl.multiple_of(i * 16, 16), 16)

    def reduce_line(chunk):
        first, taps, per = chunk
        out = []
        for h in halves:
            for j, (peer, them, _) in enumerate(h["line"]):
                dst = got1.at[h["slot"], j, pl.ds(first, taps)]
                out.append(go(part.at[pl.ds(first, taps), tile16(them), h["cols"]], dst, (peer, ch), dst))
        return out

    def reduce_group(chunk, landings):
        first, taps, per = chunk
        out = []
        for h in halves:
            for landing in landings[3 * h["slot"] : 3 * h["slot"] + 3]:
                landing.wait_recv()
            total = exact[pl.ds(first, taps), tile16(h["me"]), h["cols"]]
            for j in range(3):
                total = total + got1[h["slot"], j, pl.ds(first, taps)].astype(F32)
            h["total"][pl.ds(first, taps)] = total
            if 4 * per > taps:
                h["total"][pl.ds(first + taps, 4 * per - taps)] = jnp.zeros((4 * per - taps, 16, 128), F32)
            for j, (peer, them, _) in enumerate(h["group"]):
                dst = got2.at[h["slot"], j, pl.ds(first // 4, per)]
                out.append(go(h["total"].at[pl.ds(first + them * per, per)], dst, (peer, ch), dst))
        return out

    def reduce_mate(chunk, landings):
        first, taps, per = chunk
        out = []
        for h in halves:
            for landing in landings[3 * h["slot"] : 3 * h["slot"] + 3]:
                landing.wait_recv()
            total = h["total"][pl.ds(first + h["owner"] * per, per)]
            for j in range(3):
                total = total + got2[h["slot"], j, pl.ds(first // 4, per)]
            here = (h["slot"], pl.ds(first // 4, per))
            middle[here] = total
            out.append(go(middle.at[here], got3.at[here], mate, got3.at[here]))
        return out

    def gather_group(chunk, landings):
        first, taps, per = chunk
        out = []
        for h in halves:
            landings[h["slot"]].wait_recv()
            here = (h["slot"], pl.ds(first // 4, per))
            total = middle[here] + got3[here]
            here = (pl.ds(first + h["owner"] * per, per), tile16(h["me"]), h["cols"])
            out_ref[here] = (total * SCALE).astype(BF16)
            for peer, _, from_them in h["group"]:
                lands = out_ref.at[pl.ds(first + from_them * per, per), tile16(h["me"]), h["cols"]]
                out.append(go(out_ref.at[here], out_ref.at[here], (peer, ch), lands))
        return out

    def gather_line(chunk, landings):
        first, taps, per = chunk
        out = []
        for h in halves:
            for landing in landings[3 * h["slot"] : 3 * h["slot"] + 3]:
                landing.wait_recv()
            here = out_ref.at[pl.ds(first, taps), tile16(h["me"]), h["cols"]]
            for peer, _, from_them in h["line"]:
                lands = out_ref.at[pl.ds(first, taps), tile16(from_them), h["cols"]]
                out.append(go(here, here, (peer, ch), lands))
        return out

    lines = []
    for a, chunk in enumerate(CHUNKS):
        wgrad(a)
        lines.append(reduce_line(chunk))

    for n in range(0, CELLS, D_TILE):
        cols = pl.ds(n, D_TILE)
        value = jnp.dot(
            turned_in[...].reshape(2 * FULL, 2 * STRIDE), stacked[pl.ds(STRIDE, 2 * STRIDE), cols],
            preferred_element_type=F32,
        )
        dx[:, :, cols] = value.reshape(2, FULL, D_TILE)

    def halo_shift(d):
        def body(o, carry):
            at = pl.multiple_of(o * rows, rows)
            shift_in(ghalo[d, pl.ds(at, rows), :].astype(ROLL), at, rows, stacked, 3 * d)
            return carry

        lax.fori_loop(0, QUARTER // rows, body, 0)

    def dgrad(d):
        for n in range(0, CELLS, D_TILE):
            cols = pl.ds(n, D_TILE)
            dx[d, :, cols] += jnp.dot(
                turned_out[d], stacked[pl.ds(3 * d * STRIDE, STRIDE), cols], preferred_element_type=F32
            )

    chips, crosses = [], []

    def neighbour(d, landing):
        landing.wait_recv()
        halo_shift(d)
        dgrad(d)
        dsend[d, 0] = dx[d, twins, :].astype(BF16)
        dsend[d, 1] = dx[d, twin_others, :].astype(BF16)
        chips.append((d, go(dsend.at[d], dgot.at[d], (sp, twin), dgot.at[d])))

    def cross_over(d, chip):
        chip.wait_recv()
        dsend2[d] = (dx[d, others, :] + dgot[d, 1].astype(F32)).astype(BF16)
        crosses.append((d, go(dsend2.at[d], dgot2.at[d], (sp, other), dgot2.at[d])))

    groups = [reduce_group(chunk, line) for chunk, line in zip(CHUNKS, lines)]
    mates = [reduce_mate(CHUNKS[0], groups[0])]
    neighbour(1, g_down)
    mates.append(reduce_mate(CHUNKS[1], groups[1]))
    neighbour(0, g_up)
    mates.append(reduce_mate(CHUNKS[2], groups[2]))
    cross_over(*chips[0])
    broadcasts = [gather_group(CHUNKS[0], mates[0])]
    cross_over(*chips[1])
    broadcasts += [gather_group(chunk, mate_) for chunk, mate_ in zip(CHUNKS[1:], mates[1:])]
    finals = [gather_line(chunk, landings) for chunk, landings in zip(CHUNKS, broadcasts)]
    for d, cross in crosses:
        cross.wait_recv()
        gi_ref[d] = dx[d, mine, :] + dgot[d, 0].astype(F32) + dgot2[d].astype(F32)
    for landings in finals:
        for landing in landings:
            landing.wait_recv()
    for copy in sent:
        copy.wait_send()


COPIES = 2 + 4 + 1 + 4 + 2 + 2 + 2 + 26 * len(CHUNKS)


def local(features, weight, cotangent):
    vmem = pl.BlockSpec(memory_space=pltpu.VMEM)
    grad_input, grad_weight = pl.pallas_call(
        kernel,
        out_shape=(
            jax.ShapeDtypeStruct((2, QUARTER, CELLS), F32),
            jax.ShapeDtypeStruct((SLOTS, QUARTER, FULL), BF16),
        ),
        in_specs=[pl.BlockSpec(memory_space=pltpu.HBM)] * 3,
        out_specs=(vmem, vmem),
        scratch_shapes=[
            pltpu.VMEM((4, FULL, CELLS), BF16),
            pltpu.VMEM((2, QUARTER, CELLS), BF16),
            pltpu.VMEM((2, QUARTER, CELLS), BF16),
            pltpu.VMEM((2 * STACK, 2 * FULL), BF16),
            pltpu.VMEM((2, STACK, FULL), BF16),
            pltpu.VMEM((2, FULL, 2 * STRIDE), BF16),
            pltpu.VMEM((2, FULL, STRIDE), BF16),
            pltpu.VMEM((2 * STACK, CELLS), F32),
            pltpu.VMEM((4 * STRIDE, CELLS), BF16),
            pltpu.VMEM((2, QUARTER, CELLS), BF16),
            pltpu.VMEM((2, QUARTER, CELLS), BF16),
            pltpu.VMEM((27, QUARTER, FULL), BF16),
            pltpu.VMEM((27, QUARTER, FULL), F32),
            pltpu.VMEM((SLOTS, 16, 128), F32),
            pltpu.VMEM((SLOTS, 16, 128), F32),
            pltpu.VMEM((2, 3, 27, 16, 128), BF16),
            pltpu.VMEM((2, 3, SLOTS // 4, 16, 128), F32),
            pltpu.VMEM((2, SLOTS // 4, 16, 128), F32),
            pltpu.VMEM((2, SLOTS // 4, 16, 128), F32),
            pltpu.VMEM((2, FULL, CELLS), F32),
            pltpu.VMEM((2, 2, QUARTER, CELLS), BF16),
            pltpu.VMEM((2, 2, QUARTER, CELLS), BF16),
            pltpu.VMEM((2, QUARTER, CELLS), BF16),
            pltpu.VMEM((2, QUARTER, CELLS), BF16),
            pltpu.SemaphoreType.DMA((8,)),
            pltpu.SemaphoreType.DMA((COPIES,)),
            pltpu.SemaphoreType.DMA((COPIES,)),
        ],
        compiler_params=pltpu.CompilerParams(
            collective_id=0, has_side_effects=True, vmem_limit_bytes=62 << 20
        ),
    )(features, cotangent, weight.reshape(3, STACK, FULL))
    return grad_input, grad_weight[:27].astype(F32)


def solution(mesh):
    placed = (P("sp", "ch", None), P(None, "ch", None), P("sp", "ch", None))
    return jax.shard_map(
        local,
        mesh=mesh,
        in_specs=placed,
        out_specs=(P("sp", "ch", None), P(None, "ch", None)),
        check_vma=False,
    )
```

```python
import functools

import jax
import jax.numpy as jnp
from jax import lax
from jax.experimental import pallas as pl
from jax.experimental.pallas import tpu as pltpu
from jax.sharding import PartitionSpec as P

MESH = pl.DeviceIdType.MESH
F32, BF16 = jnp.float32, jnp.bfloat16
WIDTH = 32
CELLS = 1024
QUARTER = 64
FULL = 256
STACK = 9 * QUARTER
TILE = 256
STRIDE = 640
IN_TILE, OUT_TILE, D_TILE, ROWS = 256, 256, 256, 64
ROLL = BF16
CHUNKS = ((0, 8, 2), (8, 8, 2), (16, 11, 3))
SLOTS = 28
SCALE = 1.0 / 256.0


def wrap(value, size):
    return lax.rem(value, size)


def place():
    sp, ch = lax.axis_index("sp"), lax.axis_index("ch")
    return sp, ch, lax.div(sp, 8), lax.rem(lax.div(sp, 2), 4), lax.rem(sp, 2)


def index(x, z, y):
    return x * 8 + z * 2 + y


def roll(value, shift):
    return pltpu.roll(value, shift % CELLS, 1)


def nine(value, lane, column):
    zero = jnp.zeros_like(value)
    wide = [
        jnp.where(column <= WIDTH - 2, roll(value, -1), zero),
        value,
        jnp.where(column >= 1, roll(value, 1), zero),
    ]
    out = [jnp.where(lane < CELLS - WIDTH, roll(v, -WIDTH), zero) for v in wide]
    out += wide
    out += [jnp.where(lane >= WIDTH, roll(v, WIDTH), zero) for v in wide]
    return out


def lanes(rows):
    lane = lax.broadcasted_iota(jnp.int32, (rows, CELLS), 1)
    return lane, lax.rem(lane, WIDTH)


def shift_in(value, row, rows, stacked, plane):
    lane, column = lanes(rows)
    for s, moved in enumerate(nine(value, lane, column)):
        stacked[pl.ds(plane * STRIDE + s * QUARTER + row, rows), :] = moved.astype(BF16)


def kernel(
    f_ref, cot_ref, w_ref, gi_ref, out_ref,
    planes, edge, cot, wide_in, wide_out, turned_in, turned_out, taps_out, stacked, gedge, ghalo,
    part, exact, sum_x, sum_z, got1, got2, middle, got3, dx, dsend, dgot, dsend2, dgot2,
    local_sem, send_sem, recv_sem,
):
    sp, ch, x, z, y = place()
    other = wrap(ch + 2, 4)
    twin = lax.div(ch, 2) * 2 + wrap(ch + 1, 2)
    twin_other = wrap(twin + 2, 4)
    up, down = wrap(sp + 1, 32), wrap(sp + 31, 32)

    def near(dx_, dz_, dy_):
        return index(wrap(x + dx_, 4), wrap(z + dz_, 4), wrap(y + dy_, 2))

    barrier = pltpu.get_barrier_semaphore()
    friends = [(sp, twin), (sp, other), (up, ch), (down, ch), (up, other), (down, other)]
    friends += [(near(d, 0, 0), ch) for d in (1, 2, 3)] + [(near(0, d, 0), ch) for d in (1, 2, 3)]
    friends.append((near(0, 0, 1), ch))
    for friend in friends:
        pl.semaphore_signal(barrier, inc=1, device_id=friend, device_id_type=MESH)

    own = pl.ds(1, 2)
    mine = pl.ds(pl.multiple_of(ch * QUARTER, QUARTER), QUARTER)
    others = pl.ds(pl.multiple_of(other * QUARTER, QUARTER), QUARTER)
    twins = pl.ds(pl.multiple_of(twin * QUARTER, QUARTER), QUARTER)
    twin_others = pl.ds(pl.multiple_of(twin_other * QUARTER, QUARTER), QUARTER)

    loads = [(f_ref, planes.at[own, mine])]
    low, high = pl.ds(0, STACK), pl.ds(STACK, STACK)
    left, right = pl.ds(0, FULL), pl.ds(FULL, FULL)
    loads += [(w_ref.at[1], wide_in.at[low, left]), (w_ref.at[2], wide_in.at[low, right])]
    loads += [(w_ref.at[0], wide_in.at[high, left]), (w_ref.at[1], wide_in.at[high, right])]
    loads += [(w_ref.at[0], wide_out.at[0]), (w_ref.at[2], wide_out.at[1]), (cot_ref, cot)]
    loads = [pltpu.make_async_copy(src, dst, local_sem.at[i]) for i, (src, dst) in enumerate(loads)]
    for load in loads:
        load.start()
    loads[0].wait()
    for e, plane, inside in ((0, 2, sp < 31), (1, 1, sp > 0)):
        value = planes[plane, mine, :]
        edge[e] = jnp.where(inside, value, jnp.zeros_like(value))
    pl.semaphore_wait(barrier, len(friends))

    sent = []

    def go(src, dst, device, lands):
        i = len(sent)

        def copy_to(ref):
            return pltpu.make_async_remote_copy(
                src_ref=src, dst_ref=ref, send_sem=send_sem.at[i], recv_sem=recv_sem.at[i],
                device_id=device, device_id_type=MESH,
            )

        copy = copy_to(dst)
        copy.start()
        sent.append(copy)
        return copy_to(lands)

    def cross_plane(slot):
        return go(planes.at[slot, mine], planes.at[slot, mine], (sp, other), planes.at[slot, others])

    def pass_plane(slot, rows, arriving):
        return go(planes.at[slot, rows], planes.at[slot, rows], (sp, twin), planes.at[slot, arriving])

    def halo(e, peer, slot):
        return go(edge.at[e], planes.at[slot, mine], (peer, other), planes.at[slot, others])

    across_2 = cross_plane(2)
    halo_3 = halo(1, down, 3)
    across_1 = cross_plane(1)
    halo_0 = halo(0, up, 0)
    beside = go(planes.at[own, mine], planes.at[own, mine], (sp, twin), planes.at[own, twins])

    for load in loads[1:]:
        load.wait()
    for p in range(4):
        stacked[pl.ds(p * STRIDE + STACK, STRIDE - STACK), :] = jnp.zeros((STRIDE - STACK, CELLS), BF16)
    pad = jnp.zeros((FULL, STRIDE - STACK), BF16)
    for a, src, places in (
        (0, wide_out.at[0], (turned_in.at[0, :, pl.ds(STRIDE, STRIDE)], turned_out.at[1])),
        (1, wide_in.at[low, left], (turned_in.at[0, :, pl.ds(0, STRIDE)], turned_in.at[1, :, pl.ds(STRIDE, STRIDE)])),
        (2, wide_out.at[1], (turned_in.at[1, :, pl.ds(0, STRIDE)], turned_out.at[0])),
    ):
        for k in range(0, STACK, 128):
            n = min(128, STACK - k)
            block = src[pl.ds(k, n), :].T
            for dst in places:
                dst[:, pl.ds(k, n)] = block
        for dst in places:
            dst[:, pl.ds(STACK, STRIDE - STACK)] = pad

    across_2.wait_recv()
    value = planes[2, others, :]
    edge[2] = jnp.where(sp < 31, value, jnp.zeros_like(value))
    late_0 = go(edge.at[2], planes.at[0, others], (up, other), planes.at[0, mine])
    passed = [pass_plane(2, others, twin_others)]
    halo_3.wait_recv()
    late_3 = go(planes.at[3, others], planes.at[3, others], (sp, other), planes.at[3, mine])
    across_1.wait_recv()
    passed.append(pass_plane(1, others, twin_others))
    passes = {3: [pass_plane(3, others, twin_others)]}
    halo_0.wait_recv()
    passes[0] = [pass_plane(0, others, twin_others)]
    beside.wait_recv()
    for landing in passed:
        landing.wait_recv()

    for n in range(0, CELLS, IN_TILE):
        cols = pl.ds(n, IN_TILE)
        taps_out[:, cols] = jnp.dot(
            wide_in[...], planes[own, :, cols].reshape(2 * FULL, IN_TILE), preferred_element_type=F32
        )

    for slot, late in ((0, late_0), (3, late_3)):
        late.wait_recv()
        passes[slot].append(pass_plane(slot, mine, twins))

    def outer(d):
        for n in range(0, CELLS, OUT_TILE):
            cols = pl.ds(n, OUT_TILE)
            taps_out[pl.ds(d * STACK, STACK), cols] += jnp.dot(
                wide_out[d], planes[3 * d, :, cols], preferred_element_type=F32
            )

    rows = ROWS

    def slope(d, inside):
        def body(o, carry):
            at = pl.multiple_of(o * rows, rows)
            lane, column = lanes(rows)

            def tap(b, c):
                return taps_out[pl.ds(d * STACK + (3 * b + c) * QUARTER + at, rows), :]

            pre = None
            for c in range(3):
                total = tap(1, c)
                total = total + jnp.where(lane >= WIDTH, roll(tap(0, c), WIDTH), 0.0)
                total = total + jnp.where(lane < CELLS - WIDTH, roll(tap(2, c), -WIDTH), 0.0)
                if c == 0:
                    total = jnp.where(column >= 1, roll(total, 1), 0.0)
                if c == 2:
                    total = jnp.where(column <= WIDTH - 2, roll(total, -1), 0.0)
                pre = total if pre is None else pre + total
            s = 1.0 / (1.0 + jnp.exp(-pre))
            grad = cot[d, pl.ds(at, rows), :].astype(F32) * (s * (1.0 + pre * (1.0 - s)))
            grad = grad.astype(BF16)
            gedge[d, pl.ds(at, rows), :] = jnp.where(inside, grad, jnp.zeros_like(grad))
            shift_in(grad.astype(ROLL), at, rows, stacked, 1 + d)
            return carry

        lax.fori_loop(0, QUARTER // rows, body, 0)

    for landing in passes[0]:
        landing.wait_recv()
    outer(0)
    slope(0, sp > 0)
    g_down = go(gedge.at[0], ghalo.at[1], (down, ch), ghalo.at[1])
    for landing in passes[3]:
        landing.wait_recv()
    outer(1)
    slope(1, sp < 31)
    g_up = go(gedge.at[1], ghalo.at[0], (up, ch), ghalo.at[0])

    contract = (((1,), (1,)), ((), ()))

    def wgrad(a):
        total = None
        for d in range(2):
            term = lax.dot_general(
                stacked[pl.ds((1 + d) * STRIDE, STACK), :], planes[a + d], contract,
                preferred_element_type=F32,
            )
            total = term if total is None else total + term
        exact[pl.ds(a * 9, 9)] = total.reshape(9, QUARTER, FULL)
        part[pl.ds(a * 9, 9)] = total.astype(BF16).reshape(9, QUARTER, FULL)

    line_x = [(near(d, 0, 0), wrap(x + d, 4), wrap(x + 4 - d, 4)) for d in (1, 2, 3)]
    line_z = [(near(0, d, 0), wrap(z + d, 4), wrap(z + 4 - d, 4)) for d in (1, 2, 3)]
    halves = (
        dict(slot=0, cols=pl.ds(0, 128), me=x, line=line_x, owner=z, group=line_z, total=sum_x),
        dict(slot=1, cols=pl.ds(128, 128), me=z, line=line_z, owner=x, group=line_x, total=sum_z),
    )
    mate = (near(0, 0, 1), ch)

    def tile16(i):
        return pl.ds(pl.multiple_of(i * 16, 16), 16)

    def reduce_line(chunk):
        first, taps, per = chunk
        out = []
        for h in halves:
            for j, (peer, them, _) in enumerate(h["line"]):
                dst = got1.at[h["slot"], j, pl.ds(first, taps)]
                out.append(go(part.at[pl.ds(first, taps), tile16(them), h["cols"]], dst, (peer, ch), dst))
        return out

    def reduce_group(chunk, landings):
        first, taps, per = chunk
        out = []
        for h in halves:
            for landing in landings[3 * h["slot"] : 3 * h["slot"] + 3]:
                landing.wait_recv()
            total = exact[pl.ds(first, taps), tile16(h["me"]), h["cols"]]
            for j in range(3):
                total = total + got1[h["slot"], j, pl.ds(first, taps)].astype(F32)
            h["total"][pl.ds(first, taps)] = total
            if 4 * per > taps:
                h["total"][pl.ds(first + taps, 4 * per - taps)] = jnp.zeros((4 * per - taps, 16, 128), F32)
            for j, (peer, them, _) in enumerate(h["group"]):
                dst = got2.at[h["slot"], j, pl.ds(first // 4, per)]
                out.append(go(h["total"].at[pl.ds(first + them * per, per)], dst, (peer, ch), dst))
        return out

    def reduce_mate(chunk, landings):
        first, taps, per = chunk
        out = []
        for h in halves:
            for landing in landings[3 * h["slot"] : 3 * h["slot"] + 3]:
                landing.wait_recv()
            total = h["total"][pl.ds(first + h["owner"] * per, per)]
            for j in range(3):
                total = total + got2[h["slot"], j, pl.ds(first // 4, per)]
            here = (h["slot"], pl.ds(first // 4, per))
            middle[here] = total
            out.append(go(middle.at[here], got3.at[here], mate, got3.at[here]))
        return out

    def gather_group(chunk, landings):
        first, taps, per = chunk
        out = []
        for h in halves:
            landings[h["slot"]].wait_recv()
            here = (h["slot"], pl.ds(first // 4, per))
            total = middle[here] + got3[here]
            here = (pl.ds(first + h["owner"] * per, per), tile16(h["me"]), h["cols"])
            out_ref[here] = (total * SCALE).astype(BF16)
            for peer, _, from_them in h["group"]:
                lands = out_ref.at[pl.ds(first + from_them * per, per), tile16(h["me"]), h["cols"]]
                out.append(go(out_ref.at[here], out_ref.at[here], (peer, ch), lands))
        return out

    def gather_line(chunk, landings):
        first, taps, per = chunk
        out = []
        for h in halves:
            for landing in landings[3 * h["slot"] : 3 * h["slot"] + 3]:
                landing.wait_recv()
            here = out_ref.at[pl.ds(first, taps), tile16(h["me"]), h["cols"]]
            for peer, _, from_them in h["line"]:
                lands = out_ref.at[pl.ds(first, taps), tile16(from_them), h["cols"]]
                out.append(go(here, here, (peer, ch), lands))
        return out

    lines = []
    for a in range(3):
        wgrad(a)
        while len(lines) < len(CHUNKS) and sum(CHUNKS[len(lines)][:2]) <= 9 * a + 9:
            lines.append(reduce_line(CHUNKS[len(lines)]))

    for n in range(0, CELLS, D_TILE):
        cols = pl.ds(n, D_TILE)
        value = jnp.dot(
            turned_in[...].reshape(2 * FULL, 2 * STRIDE), stacked[pl.ds(STRIDE, 2 * STRIDE), cols],
            preferred_element_type=F32,
        )
        dx[:, :, cols] = value.reshape(2, FULL, D_TILE)

    def halo_shift(d):
        def body(o, carry):
            at = pl.multiple_of(o * rows, rows)
            shift_in(ghalo[d, pl.ds(at, rows), :].astype(ROLL), at, rows, stacked, 3 * d)
            return carry

        lax.fori_loop(0, QUARTER // rows, body, 0)

    def dgrad(d):
        for n in range(0, CELLS, D_TILE):
            cols = pl.ds(n, D_TILE)
            dx[d, :, cols] += jnp.dot(
                turned_out[d], stacked[pl.ds(3 * d * STRIDE, STRIDE), cols], preferred_element_type=F32
            )

    chips, crosses = [], []

    def neighbour(d, landing):
        landing.wait_recv()
        halo_shift(d)
        dgrad(d)
        dsend[d, 0] = dx[d, twins, :].astype(BF16)
        dsend[d, 1] = dx[d, twin_others, :].astype(BF16)
        chips.append((d, go(dsend.at[d], dgot.at[d], (sp, twin), dgot.at[d])))

    def cross_over(d, chip):
        chip.wait_recv()
        dsend2[d] = (dx[d, others, :] + dgot[d, 1].astype(F32)).astype(BF16)
        crosses.append((d, go(dsend2.at[d], dgot2.at[d], (sp, other), dgot2.at[d])))

    groups = [reduce_group(chunk, line) for chunk, line in zip(CHUNKS, lines)]
    n = len(CHUNKS)
    mates = [reduce_mate(CHUNKS[i], groups[i]) for i in range((n + 1) // 3)]
    neighbour(1, g_down)
    mates += [reduce_mate(CHUNKS[i], groups[i]) for i in range(len(mates), n - 1)]
    neighbour(0, g_up)
    mates += [reduce_mate(CHUNKS[i], groups[i]) for i in range(len(mates), n)]
    cross_over(*chips[0])
    broadcasts = [gather_group(CHUNKS[0], mates[0])]
    cross_over(*chips[1])
    broadcasts += [gather_group(chunk, mate_) for chunk, mate_ in zip(CHUNKS[1:], mates[1:])]
    finals = [gather_line(chunk, landings) for chunk, landings in zip(CHUNKS, broadcasts)]
    for d, cross in crosses:
        cross.wait_recv()
        gi_ref[d] = dx[d, mine, :] + dgot[d, 0].astype(F32) + dgot2[d].astype(F32)
    for landings in finals:
        for landing in landings:
            landing.wait_recv()
    for copy in sent:
        copy.wait_send()


COPIES = 5 + 2 + 6 + 2 + 2 + 2 + 26 * len(CHUNKS)


def local(features, weight, cotangent):
    vmem = pl.BlockSpec(memory_space=pltpu.VMEM)
    grad_input, grad_weight = pl.pallas_call(
        kernel,
        out_shape=(
            jax.ShapeDtypeStruct((2, QUARTER, CELLS), F32),
            jax.ShapeDtypeStruct((SLOTS, QUARTER, FULL), BF16),
        ),
        in_specs=[pl.BlockSpec(memory_space=pltpu.HBM)] * 3,
        out_specs=(vmem, vmem),
        scratch_shapes=[
            pltpu.VMEM((4, FULL, CELLS), BF16),
            pltpu.VMEM((3, QUARTER, CELLS), BF16),
            pltpu.VMEM((2, QUARTER, CELLS), BF16),
            pltpu.VMEM((2 * STACK, 2 * FULL), BF16),
            pltpu.VMEM((2, STACK, FULL), BF16),
            pltpu.VMEM((2, FULL, 2 * STRIDE), BF16),
            pltpu.VMEM((2, FULL, STRIDE), BF16),
            pltpu.VMEM((2 * STACK, CELLS), F32),
            pltpu.VMEM((4 * STRIDE, CELLS), BF16),
            pltpu.VMEM((2, QUARTER, CELLS), BF16),
            pltpu.VMEM((2, QUARTER, CELLS), BF16),
            pltpu.VMEM((27, QUARTER, FULL), BF16),
            pltpu.VMEM((27, QUARTER, FULL), F32),
            pltpu.VMEM((SLOTS, 16, 128), F32),
            pltpu.VMEM((SLOTS, 16, 128), F32),
            pltpu.VMEM((2, 3, 27, 16, 128), BF16),
            pltpu.VMEM((2, 3, SLOTS // 4, 16, 128), F32),
            pltpu.VMEM((2, SLOTS // 4, 16, 128), F32),
            pltpu.VMEM((2, SLOTS // 4, 16, 128), F32),
            pltpu.VMEM((2, FULL, CELLS), F32),
            pltpu.VMEM((2, 2, QUARTER, CELLS), BF16),
            pltpu.VMEM((2, 2, QUARTER, CELLS), BF16),
            pltpu.VMEM((2, QUARTER, CELLS), BF16),
            pltpu.VMEM((2, QUARTER, CELLS), BF16),
            pltpu.SemaphoreType.DMA((8,)),
            pltpu.SemaphoreType.DMA((COPIES,)),
            pltpu.SemaphoreType.DMA((COPIES,)),
        ],
        compiler_params=pltpu.CompilerParams(
            collective_id=0, has_side_effects=True, vmem_limit_bytes=48 << 20
        ),
    )(*(pltpu.with_memory_space_constraint(v, pltpu.HBM) for v in (features, cotangent, weight.reshape(3, STACK, FULL))))
    return grad_input, grad_weight[:27].astype(F32)


def solution(mesh):
    placed = (P("sp", "ch", None), P(None, "ch", None), P("sp", "ch", None))
    return jax.shard_map(
        local,
        mesh=mesh,
        in_specs=placed,
        out_specs=(P("sp", "ch", None), P(None, "ch", None)),
        check_vma=False,
    )
```

```python
import functools

import jax
import jax.numpy as jnp
from jax import lax
from jax.experimental import pallas as pl
from jax.experimental.pallas import tpu as pltpu
from jax.sharding import PartitionSpec as P

MESH = pl.DeviceIdType.MESH
F32, BF16 = jnp.float32, jnp.bfloat16
WIDTH = 32
CELLS = 1024
QUARTER = 64
FULL = 256
STACK = 9 * QUARTER
BAND = 3 * QUARTER
TILE = 256
STRIDE = 640
IN_TILE, OUT_TILE, D_TILE, ROWS = 256, 256, 256, 64
ROLL = BF16
CHUNKS = ((0, 8, 2), (8, 8, 2), (16, 11, 3))
SLOTS = 28
SCALE = 1.0 / 256.0


def wrap(value, size):
    return lax.rem(value, size)


def place():
    sp, ch = lax.axis_index("sp"), lax.axis_index("ch")
    return sp, ch, lax.div(sp, 8), lax.rem(lax.div(sp, 2), 4), lax.rem(sp, 2)


def index(x, z, y):
    return x * 8 + z * 2 + y


def roll(value, shift):
    return pltpu.roll(value, shift % CELLS, 1)


def nine(value, lane, column):
    zero = jnp.zeros_like(value)
    wide = [
        jnp.where(column <= WIDTH - 2, roll(value, -1), zero),
        value,
        jnp.where(column >= 1, roll(value, 1), zero),
    ]
    out = [jnp.where(lane < CELLS - WIDTH, roll(v, -WIDTH), zero) for v in wide]
    out += wide
    out += [jnp.where(lane >= WIDTH, roll(v, WIDTH), zero) for v in wide]
    return out


def lanes(rows):
    lane = lax.broadcasted_iota(jnp.int32, (rows, CELLS), 1)
    return lane, lax.rem(lane, WIDTH)


def shift_in(value, row, rows, stacked, plane):
    lane, column = lanes(rows)
    for s, moved in enumerate(nine(value, lane, column)):
        stacked[pl.ds(plane * STRIDE + s * QUARTER + row, rows), :] = moved.astype(BF16)


def kernel(
    f_ref, cot_ref, w_ref, gi_ref, out_ref,
    high, edge, cot, wide_in, wide_out, turned_in, turned_out, taps_out, stacked, gedge, ghalo,
    part, exact, sum_x, sum_z, got1, got2, middle, got3, dx, dsend, dgot, dsend2, dgot2,
    local_sem, send_sem, recv_sem,
):
    planes = high.at[1]
    sp, ch, x, z, y = place()
    other = wrap(ch + 2, 4)
    twin = lax.div(ch, 2) * 2 + wrap(ch + 1, 2)
    twin_other = wrap(twin + 2, 4)
    up, down = wrap(sp + 1, 32), wrap(sp + 31, 32)

    def near(dx_, dz_, dy_):
        return index(wrap(x + dx_, 4), wrap(z + dz_, 4), wrap(y + dy_, 2))

    barrier = pltpu.get_barrier_semaphore()
    friends = [(sp, twin), (sp, other), (up, ch), (down, ch), (up, other), (down, other)]
    friends += [(near(d, 0, 0), ch) for d in (1, 2, 3)] + [(near(0, d, 0), ch) for d in (1, 2, 3)]
    friends.append((near(0, 0, 1), ch))
    for friend in friends:
        pl.semaphore_signal(barrier, inc=1, device_id=friend, device_id_type=MESH)

    own = pl.ds(1, 2)
    mine = pl.ds(pl.multiple_of(ch * QUARTER, QUARTER), QUARTER)
    others = pl.ds(pl.multiple_of(other * QUARTER, QUARTER), QUARTER)
    twins = pl.ds(pl.multiple_of(twin * QUARTER, QUARTER), QUARTER)
    twin_others = pl.ds(pl.multiple_of(twin_other * QUARTER, QUARTER), QUARTER)

    loads = [(f_ref, planes.at[own, mine]), (cot_ref, cot)]
    for b in range(3):
        rows_b = pl.ds(b * BAND, BAND)
        for d in range(2):
            for p in range(2):
                place_in = wide_in.at[pl.ds(d * BAND, BAND), pl.ds((2 * b + p) * FULL, FULL)]
                loads.append((w_ref.at[p + 1 - d, rows_b], place_in))
            loads.append((w_ref.at[2 * d, rows_b], wide_out.at[d, :, pl.ds(b * FULL, FULL)]))
    loads = [pltpu.make_async_copy(src, dst, local_sem.at[i]) for i, (src, dst) in enumerate(loads)]
    for load in loads:
        load.start()
    loads[0].wait()
    for e, plane, inside in ((0, 2, sp < 31), (1, 1, sp > 0)):
        value = planes[plane, mine, :]
        edge[e] = jnp.where(inside, value, jnp.zeros_like(value))

    def shift_rows(slot, rows):
        value = planes[slot, rows, :]
        lane, _ = lanes(QUARTER)
        zero = jnp.zeros_like(value)
        high[0, slot, rows, :] = jnp.where(lane >= WIDTH, roll(value, WIDTH), zero)
        high[2, slot, rows, :] = jnp.where(lane < CELLS - WIDTH, roll(value, -WIDTH), zero)

    pl.semaphore_wait(barrier, len(friends))

    sent = []

    def go(src, dst, device, lands):
        i = len(sent)

        def copy_to(ref):
            return pltpu.make_async_remote_copy(
                src_ref=src, dst_ref=ref, send_sem=send_sem.at[i], recv_sem=recv_sem.at[i],
                device_id=device, device_id_type=MESH,
            )

        copy = copy_to(dst)
        copy.start()
        sent.append(copy)
        return copy_to(lands)

    def cross_plane(slot):
        return go(planes.at[slot, mine], planes.at[slot, mine], (sp, other), planes.at[slot, others])

    def pass_plane(slot, rows, arriving):
        return go(planes.at[slot, rows], planes.at[slot, rows], (sp, twin), planes.at[slot, arriving])

    def halo(e, peer, slot):
        return go(edge.at[e], planes.at[slot, mine], (peer, other), planes.at[slot, others])

    across_2 = cross_plane(2)
    halo_3 = halo(1, down, 3)
    across_1 = cross_plane(1)
    halo_0 = halo(0, up, 0)
    beside = go(planes.at[own, mine], planes.at[own, mine], (sp, twin), planes.at[own, twins])

    for load in loads[1:]:
        load.wait()
    for p in range(4):
        stacked[pl.ds(p * STRIDE + STACK, STRIDE - STACK), :] = jnp.zeros((STRIDE - STACK, CELLS), BF16)
    pad = jnp.zeros((FULL, STRIDE - STACK), BF16)
    for a, places in (
        (0, (turned_in.at[0, :, pl.ds(STRIDE, STRIDE)], turned_out.at[1])),
        (1, (turned_in.at[0, :, pl.ds(0, STRIDE)], turned_in.at[1, :, pl.ds(STRIDE, STRIDE)])),
        (2, (turned_in.at[1, :, pl.ds(0, STRIDE)], turned_out.at[0])),
    ):
        for s in range(9):
            b, rows_c = s // 3, pl.ds(s % 3 * QUARTER, QUARTER)
            if a == 1:
                block = wide_in[rows_c, pl.ds(2 * b * FULL, FULL)].T
            else:
                block = wide_out[a // 2, rows_c, pl.ds(b * FULL, FULL)].T
            for dst in places:
                dst[:, pl.ds(s * QUARTER, QUARTER)] = block
        for dst in places:
            dst[:, pl.ds(STACK, STRIDE - STACK)] = pad
    for slot in (1, 2):
        shift_rows(slot, mine)

    across_2.wait_recv()
    value = planes[2, others, :]
    edge[2] = jnp.where(sp < 31, value, jnp.zeros_like(value))
    late_0 = go(edge.at[2], planes.at[0, others], (up, other), planes.at[0, mine])
    passed = [pass_plane(2, others, twin_others)]
    halo_3.wait_recv()
    late_3 = go(planes.at[3, others], planes.at[3, others], (sp, other), planes.at[3, mine])
    across_1.wait_recv()
    passed.append(pass_plane(1, others, twin_others))
    passes = {3: [pass_plane(3, others, twin_others)]}
    halo_0.wait_recv()
    passes[0] = [pass_plane(0, others, twin_others)]
    for slot in (2, 1, 3, 0):
        shift_rows(slot, others)
    beside.wait_recv()
    for slot in (1, 2):
        shift_rows(slot, twins)
    for slot, landing in zip((2, 1), passed):
        landing.wait_recv()
        shift_rows(slot, twin_others)

    for n in range(0, CELLS, IN_TILE):
        cols = pl.ds(n, IN_TILE)
        value = jnp.concatenate([high[b, own, :, cols].reshape(2 * FULL, IN_TILE) for b in range(3)], axis=0)
        taps_out[:, cols] = jnp.dot(wide_in[...], value, preferred_element_type=F32)
    for slot in (3, 0):
        passes[slot][0].wait_recv()
        shift_rows(slot, twin_others)

    for slot, late in ((0, late_0), (3, late_3)):
        late.wait_recv()
        passes[slot].append(pass_plane(slot, mine, twins))
        shift_rows(slot, mine)

    def outer(d):
        for n in range(0, CELLS, OUT_TILE):
            cols = pl.ds(n, OUT_TILE)
            value = high[:, 3 * d, :, cols].reshape(3 * FULL, OUT_TILE)
            taps_out[pl.ds(d * BAND, BAND), cols] += jnp.dot(wide_out[d], value, preferred_element_type=F32)

    rows = ROWS

    def slope(d, inside):
        def body(o, carry):
            at = pl.multiple_of(o * rows, rows)
            lane, column = lanes(rows)

            def tap(c):
                return taps_out[pl.ds(d * BAND + c * QUARTER + at, rows), :]

            pre = tap(1)
            pre = pre + jnp.where(column >= 1, roll(tap(0), 1), 0.0)
            pre = pre + jnp.where(column <= WIDTH - 2, roll(tap(2), -1), 0.0)
            s = 1.0 / (1.0 + jnp.exp(-pre))
            grad = cot[d, pl.ds(at, rows), :].astype(F32) * (s * (1.0 + pre * (1.0 - s)))
            grad = grad.astype(BF16)
            gedge[d, pl.ds(at, rows), :] = jnp.where(inside, grad, jnp.zeros_like(grad))
            shift_in(grad.astype(ROLL), at, rows, stacked, 1 + d)
            return carry

        lax.fori_loop(0, QUARTER // rows, body, 0)

    passes[0][1].wait_recv()
    shift_rows(0, twins)
    outer(0)
    slope(0, sp > 0)
    g_down = go(gedge.at[0], ghalo.at[1], (down, ch), ghalo.at[1])
    passes[3][1].wait_recv()
    shift_rows(3, twins)
    outer(1)
    slope(1, sp < 31)
    g_up = go(gedge.at[1], ghalo.at[0], (up, ch), ghalo.at[0])

    contract = (((1,), (1,)), ((), ()))

    def wgrad(a):
        total = None
        for d in range(2):
            term = lax.dot_general(
                stacked[pl.ds((1 + d) * STRIDE, STACK), :], planes[a + d], contract,
                preferred_element_type=F32,
            )
            total = term if total is None else total + term
        exact[pl.ds(a * 9, 9)] = total.reshape(9, QUARTER, FULL)
        part[pl.ds(a * 9, 9)] = total.astype(BF16).reshape(9, QUARTER, FULL)

    line_x = [(near(d, 0, 0), wrap(x + d, 4), wrap(x + 4 - d, 4)) for d in (2, 1, 3)]
    line_z = [(near(0, d, 0), wrap(z + d, 4), wrap(z + 4 - d, 4)) for d in (2, 1, 3)]
    halves = (
        dict(slot=0, cols=pl.ds(0, 128), me=x, line=line_x, owner=z, group=line_z, total=sum_x),
        dict(slot=1, cols=pl.ds(128, 128), me=z, line=line_z, owner=x, group=line_x, total=sum_z),
    )
    mate = (near(0, 0, 1), ch)

    def tile16(i):
        return pl.ds(pl.multiple_of(i * 16, 16), 16)

    def reduce_line(chunk):
        first, taps, per = chunk
        out = []
        for h in halves:
            for j, (peer, them, _) in enumerate(h["line"]):
                dst = got1.at[h["slot"], j, pl.ds(first, taps)]
                out.append(go(part.at[pl.ds(first, taps), tile16(them), h["cols"]], dst, (peer, ch), dst))
        return out

    def reduce_group(chunk, landings):
        first, taps, per = chunk
        out = []
        for h in halves:
            for landing in landings[3 * h["slot"] : 3 * h["slot"] + 3]:
                landing.wait_recv()
            total = exact[pl.ds(first, taps), tile16(h["me"]), h["cols"]]
            for j in range(3):
                total = total + got1[h["slot"], j, pl.ds(first, taps)].astype(F32)
            h["total"][pl.ds(first, taps)] = total
            if 4 * per > taps:
                h["total"][pl.ds(first + taps, 4 * per - taps)] = jnp.zeros((4 * per - taps, 16, 128), F32)
            for j, (peer, them, _) in enumerate(h["group"]):
                dst = got2.at[h["slot"], j, pl.ds(first // 4, per)]
                out.append(go(h["total"].at[pl.ds(first + them * per, per)], dst, (peer, ch), dst))
        return out

    def reduce_mate(chunk, landings):
        first, taps, per = chunk
        out = []
        for h in halves:
            for landing in landings[3 * h["slot"] : 3 * h["slot"] + 3]:
                landing.wait_recv()
            total = h["total"][pl.ds(first + h["owner"] * per, per)]
            for j in range(3):
                total = total + got2[h["slot"], j, pl.ds(first // 4, per)]
            here = (h["slot"], pl.ds(first // 4, per))
            middle[here] = total
            out.append(go(middle.at[here], got3.at[here], mate, got3.at[here]))
        return out

    def gather_group(chunk, landings):
        first, taps, per = chunk
        out = []
        for h in halves:
            landings[h["slot"]].wait_recv()
            here = (h["slot"], pl.ds(first // 4, per))
            total = middle[here] + got3[here]
            here = (pl.ds(first + h["owner"] * per, per), tile16(h["me"]), h["cols"])
            out_ref[here] = (total * SCALE).astype(BF16)
            for peer, _, from_them in h["group"]:
                lands = out_ref.at[pl.ds(first + from_them * per, per), tile16(h["me"]), h["cols"]]
                out.append(go(out_ref.at[here], out_ref.at[here], (peer, ch), lands))
        return out

    def gather_line(chunk, landings):
        first, taps, per = chunk
        out = []
        for h in halves:
            for landing in landings[3 * h["slot"] : 3 * h["slot"] + 3]:
                landing.wait_recv()
            here = out_ref.at[pl.ds(first, taps), tile16(h["me"]), h["cols"]]
            for peer, _, from_them in h["line"]:
                lands = out_ref.at[pl.ds(first, taps), tile16(from_them), h["cols"]]
                out.append(go(here, here, (peer, ch), lands))
        return out

    lines = []
    for a in range(3):
        wgrad(a)
        while len(lines) < len(CHUNKS) and sum(CHUNKS[len(lines)][:2]) <= 9 * a + 9:
            lines.append(reduce_line(CHUNKS[len(lines)]))

    for n in range(0, CELLS, D_TILE):
        cols = pl.ds(n, D_TILE)
        value = jnp.dot(
            turned_in[...].reshape(2 * FULL, 2 * STRIDE), stacked[pl.ds(STRIDE, 2 * STRIDE), cols],
            preferred_element_type=F32,
        )
        dx[:, :, cols] = value.reshape(2, FULL, D_TILE)

    def halo_shift(d):
        def body(o, carry):
            at = pl.multiple_of(o * rows, rows)
            shift_in(ghalo[d, pl.ds(at, rows), :].astype(ROLL), at, rows, stacked, 3 * d)
            return carry

        lax.fori_loop(0, QUARTER // rows, body, 0)

    def dgrad(d):
        for n in range(0, CELLS, D_TILE):
            cols = pl.ds(n, D_TILE)
            dx[d, :, cols] += jnp.dot(
                turned_out[d], stacked[pl.ds(3 * d * STRIDE, STRIDE), cols], preferred_element_type=F32
            )

    chips, crosses = [], []

    def neighbour(d, landing):
        landing.wait_recv()
        halo_shift(d)
        dgrad(d)
        dsend[d, 0] = dx[d, twins, :].astype(BF16)
        dsend[d, 1] = dx[d, twin_others, :].astype(BF16)
        chips.append((d, go(dsend.at[d], dgot.at[d], (sp, twin), dgot.at[d])))

    def cross_over(d, chip):
        chip.wait_recv()
        dsend2[d] = (dx[d, others, :] + dgot[d, 1].astype(F32)).astype(BF16)
        crosses.append((d, go(dsend2.at[d], dgot2.at[d], (sp, other), dgot2.at[d])))

    groups = [reduce_group(chunk, line) for chunk, line in zip(CHUNKS, lines)]
    n = len(CHUNKS)
    mates = [reduce_mate(CHUNKS[i], groups[i]) for i in range((n + 1) // 3)]
    neighbour(1, g_down)
    mates += [reduce_mate(CHUNKS[i], groups[i]) for i in range(len(mates), n - 1)]
    neighbour(0, g_up)
    mates += [reduce_mate(CHUNKS[i], groups[i]) for i in range(len(mates), n)]
    cross_over(*chips[0])
    broadcasts = [gather_group(CHUNKS[0], mates[0])]
    cross_over(*chips[1])
    broadcasts += [gather_group(chunk, mate_) for chunk, mate_ in zip(CHUNKS[1:], mates[1:])]
    finals = [gather_line(chunk, landings) for chunk, landings in zip(CHUNKS, broadcasts)]
    for d, cross in crosses:
        cross.wait_recv()
        gi_ref[d] = dx[d, mine, :] + dgot[d, 0].astype(F32) + dgot2[d].astype(F32)
    for landings in finals:
        for landing in landings:
            landing.wait_recv()
    for copy in sent:
        copy.wait_send()


COPIES = 5 + 2 + 6 + 2 + 2 + 2 + 26 * len(CHUNKS)


def local(features, weight, cotangent):
    vmem = pl.BlockSpec(memory_space=pltpu.VMEM)
    grad_input, grad_weight = pl.pallas_call(
        kernel,
        out_shape=(
            jax.ShapeDtypeStruct((2, QUARTER, CELLS), F32),
            jax.ShapeDtypeStruct((SLOTS, QUARTER, FULL), BF16),
        ),
        in_specs=[pl.BlockSpec(memory_space=pltpu.HBM)] * 3,
        out_specs=(vmem, vmem),
        scratch_shapes=[
            pltpu.VMEM((3, 4, FULL, CELLS), BF16),
            pltpu.VMEM((3, QUARTER, CELLS), BF16),
            pltpu.VMEM((2, QUARTER, CELLS), BF16),
            pltpu.VMEM((2 * BAND, 6 * FULL), BF16),
            pltpu.VMEM((2, BAND, 3 * FULL), BF16),
            pltpu.VMEM((2, FULL, 2 * STRIDE), BF16),
            pltpu.VMEM((2, FULL, STRIDE), BF16),
            pltpu.VMEM((2 * BAND, CELLS), F32),
            pltpu.VMEM((4 * STRIDE, CELLS), BF16),
            pltpu.VMEM((2, QUARTER, CELLS), BF16),
            pltpu.VMEM((2, QUARTER, CELLS), BF16),
            pltpu.VMEM((27, QUARTER, FULL), BF16),
            pltpu.VMEM((27, QUARTER, FULL), F32),
            pltpu.VMEM((SLOTS, 16, 128), F32),
            pltpu.VMEM((SLOTS, 16, 128), F32),
            pltpu.VMEM((2, 3, 27, 16, 128), BF16),
            pltpu.VMEM((2, 3, SLOTS // 4, 16, 128), F32),
            pltpu.VMEM((2, SLOTS // 4, 16, 128), F32),
            pltpu.VMEM((2, SLOTS // 4, 16, 128), F32),
            pltpu.VMEM((2, FULL, CELLS), F32),
            pltpu.VMEM((2, 2, QUARTER, CELLS), BF16),
            pltpu.VMEM((2, 2, QUARTER, CELLS), BF16),
            pltpu.VMEM((2, QUARTER, CELLS), BF16),
            pltpu.VMEM((2, QUARTER, CELLS), BF16),
            pltpu.SemaphoreType.DMA((20,)),
            pltpu.SemaphoreType.DMA((COPIES,)),
            pltpu.SemaphoreType.DMA((COPIES,)),
        ],
        compiler_params=pltpu.CompilerParams(
            collective_id=0, has_side_effects=True, vmem_limit_bytes=48 << 20
        ),
    )(*(pltpu.with_memory_space_constraint(v, pltpu.HBM) for v in (features, cotangent, weight.reshape(3, STACK, FULL))))
    return grad_input, grad_weight[:27].astype(F32)


def solution(mesh):
    placed = (P("sp", "ch", None), P(None, "ch", None), P("sp", "ch", None))
    return jax.shard_map(
        local,
        mesh=mesh,
        in_specs=placed,
        out_specs=(P("sp", "ch", None), P(None, "ch", None)),
        check_vma=False,
    )
```

```python
import functools

import jax
import jax.numpy as jnp
from jax import lax
from jax.experimental import pallas as pl
from jax.experimental.pallas import tpu as pltpu
from jax.sharding import PartitionSpec as P

MESH = pl.DeviceIdType.MESH
F32, BF16 = jnp.float32, jnp.bfloat16
WIDTH = 32
CELLS = 1024
QUARTER = 64
HALF = 32
FULL = 256
STACK = 9 * QUARTER
BAND = 3 * QUARTER
TILE = 256
STRIDE = 640
IN_TILE, OUT_TILE, D_TILE, ROWS = 256, 256, 256, 64
ROLL = BF16
CHUNKS = ((0, 8, 2), (8, 8, 2), (16, 11, 3))
SLOTS = 28
SCALE = 1.0 / 256.0


def wrap(value, size):
    return lax.rem(value, size)


def place():
    sp, ch = lax.axis_index("sp"), lax.axis_index("ch")
    return sp, ch, lax.div(sp, 8), lax.rem(lax.div(sp, 2), 4), lax.rem(sp, 2)


def index(x, z, y):
    return x * 8 + z * 2 + y


def roll(value, shift):
    return pltpu.roll(value, shift % CELLS, 1)


def nine(value, lane, column):
    zero = jnp.zeros_like(value)
    wide = [
        jnp.where(column <= WIDTH - 2, roll(value, -1), zero),
        value,
        jnp.where(column >= 1, roll(value, 1), zero),
    ]
    out = [jnp.where(lane < CELLS - WIDTH, roll(v, -WIDTH), zero) for v in wide]
    out += wide
    out += [jnp.where(lane >= WIDTH, roll(v, WIDTH), zero) for v in wide]
    return out


def lanes(rows):
    lane = lax.broadcasted_iota(jnp.int32, (rows, CELLS), 1)
    return lane, lax.rem(lane, WIDTH)


def shift_in(value, row, rows, stacked, plane):
    lane, column = lanes(rows)
    for s, moved in enumerate(nine(value, lane, column)):
        stacked[pl.ds(plane * STRIDE + s * QUARTER + row, rows), :] = moved.astype(BF16)


def kernel(
    f_ref, cot_ref, w_ref, gi_ref, out_ref,
    high, edge, cot, wide_in, wide_out, turned_in, turned_out, taps_out, stacked, gedge, ghalo,
    part, exact, sum_x, sum_z, got1, got2, middle, got3, dx, dsend, dgot, dsend2, dgot2,
    local_sem, send_sem, recv_sem,
):
    planes = high.at[1]
    sp, ch, x, z, y = place()
    other = wrap(ch + 2, 4)
    twin = lax.div(ch, 2) * 2 + wrap(ch + 1, 2)
    twin_other = wrap(twin + 2, 4)
    up, down = wrap(sp + 1, 32), wrap(sp + 31, 32)

    def near(dx_, dz_, dy_):
        return index(wrap(x + dx_, 4), wrap(z + dz_, 4), wrap(y + dy_, 2))

    barrier = pltpu.get_barrier_semaphore()
    friends = [(sp, twin), (sp, other), (up, ch), (down, ch), (up, other), (down, other)]
    friends += [(near(d, 0, 0), ch) for d in (1, 2, 3)] + [(near(0, d, 0), ch) for d in (1, 2, 3)]
    friends.append((near(0, 0, 1), ch))
    for friend in friends:
        pl.semaphore_signal(barrier, inc=1, device_id=friend, device_id_type=MESH)

    own = pl.ds(1, 2)
    mine = pl.ds(pl.multiple_of(ch * QUARTER, QUARTER), QUARTER)
    others = pl.ds(pl.multiple_of(other * QUARTER, QUARTER), QUARTER)
    twins = pl.ds(pl.multiple_of(twin * QUARTER, QUARTER), QUARTER)
    twin_others = pl.ds(pl.multiple_of(twin_other * QUARTER, QUARTER), QUARTER)

    loads = [(f_ref, planes.at[own, mine]), (cot_ref, cot)]
    for b in range(3):
        rows_b = pl.ds(b * BAND, BAND)
        for d in range(2):
            for p in range(2):
                place_in = wide_in.at[pl.ds(d * BAND, BAND), pl.ds((2 * b + p) * FULL, FULL)]
                loads.append((w_ref.at[p + 1 - d, rows_b], place_in))
            loads.append((w_ref.at[2 * d, rows_b], wide_out.at[d, :, pl.ds(b * FULL, FULL)]))
    loads = [pltpu.make_async_copy(src, dst, local_sem.at[i]) for i, (src, dst) in enumerate(loads)]
    for load in loads:
        load.start()
    loads[0].wait()
    for e, plane, inside in ((0, 2, sp < 31), (1, 1, sp > 0)):
        value = planes[plane, mine, :]
        edge[e] = jnp.where(inside, value, jnp.zeros_like(value))

    def shift_rows(slot, rows):
        value = planes[slot, rows, :]
        lane, _ = lanes(QUARTER)
        zero = jnp.zeros_like(value)
        high[0, slot, rows, :] = jnp.where(lane >= WIDTH, roll(value, WIDTH), zero)
        high[2, slot, rows, :] = jnp.where(lane < CELLS - WIDTH, roll(value, -WIDTH), zero)

    pl.semaphore_wait(barrier, len(friends))

    sent = []

    def go(src, dst, device, lands):
        i = len(sent)

        def copy_to(ref):
            return pltpu.make_async_remote_copy(
                src_ref=src, dst_ref=ref, send_sem=send_sem.at[i], recv_sem=recv_sem.at[i],
                device_id=device, device_id_type=MESH,
            )

        copy = copy_to(dst)
        copy.start()
        sent.append(copy)
        return copy_to(lands)

    def half(quarter, k):
        return pl.ds(pl.multiple_of(quarter * QUARTER + k * HALF, HALF), HALF)

    def cross_plane(slot):
        return go(planes.at[slot, mine], planes.at[slot, mine], (sp, other), planes.at[slot, others])

    def cross_half(slot, k):
        here = planes.at[slot, half(ch, k)]
        return go(here, here, (sp, other), planes.at[slot, half(other, k)])

    def halo_half(e, peer, slot, k):
        src = edge.at[e, pl.ds(k * HALF, HALF)]
        return go(src, planes.at[slot, half(ch, k)], (peer, other), planes.at[slot, half(other, k)])

    def pass_plane(slot, rows, arriving):
        return go(planes.at[slot, rows], planes.at[slot, rows], (sp, twin), planes.at[slot, arriving])

    def halo(e, peer, slot):
        return go(edge.at[e], planes.at[slot, mine], (peer, other), planes.at[slot, others])

    across_2, halo_3 = [], []
    for k in range(2):
        across_2.append(cross_half(2, k))
        halo_3.append(halo_half(1, down, 3, k))
    across_1 = cross_plane(1)
    halo_0 = halo(0, up, 0)
    beside = go(planes.at[own, mine], planes.at[own, mine], (sp, twin), planes.at[own, twins])

    for load in loads[1:]:
        load.wait()
    for p in range(4):
        stacked[pl.ds(p * STRIDE + STACK, STRIDE - STACK), :] = jnp.zeros((STRIDE - STACK, CELLS), BF16)
    pad = jnp.zeros((FULL, STRIDE - STACK), BF16)
    for a, places in (
        (0, (turned_in.at[0, :, pl.ds(STRIDE, STRIDE)], turned_out.at[1])),
        (1, (turned_in.at[0, :, pl.ds(0, STRIDE)], turned_in.at[1, :, pl.ds(STRIDE, STRIDE)])),
        (2, (turned_in.at[1, :, pl.ds(0, STRIDE)], turned_out.at[0])),
    ):
        for s in range(9):
            b, rows_c = s // 3, pl.ds(s % 3 * QUARTER, QUARTER)
            if a == 1:
                block = wide_in[rows_c, pl.ds(2 * b * FULL, FULL)].T
            else:
                block = wide_out[a // 2, rows_c, pl.ds(b * FULL, FULL)].T
            for dst in places:
                dst[:, pl.ds(s * QUARTER, QUARTER)] = block
        for dst in places:
            dst[:, pl.ds(STACK, STRIDE - STACK)] = pad
    for slot in (1, 2):
        shift_rows(slot, mine)

    late_0, late_3 = [], []
    for k in range(2):
        strip = pl.ds(k * HALF, HALF)
        across_2[k].wait_recv()
        value = planes[2, half(other, k), :]
        edge[2, strip] = jnp.where(sp < 31, value, jnp.zeros_like(value))
        late_0.append(go(edge.at[2, strip], planes.at[0, half(other, k)], (up, other), planes.at[0, half(ch, k)]))
        halo_3[k].wait_recv()
        here = planes.at[3, half(other, k)]
        late_3.append(go(here, here, (sp, other), planes.at[3, half(ch, k)]))
    passed = [pass_plane(2, others, twin_others)]
    across_1.wait_recv()
    passed.append(pass_plane(1, others, twin_others))
    passes = {3: [pass_plane(3, others, twin_others)]}
    halo_0.wait_recv()
    passes[0] = [pass_plane(0, others, twin_others)]
    for slot in (2, 1, 3, 0):
        shift_rows(slot, others)
    beside.wait_recv()
    for slot in (1, 2):
        shift_rows(slot, twins)
    for slot, landing in zip((2, 1), passed):
        landing.wait_recv()
        shift_rows(slot, twin_others)

    for n in range(0, CELLS, IN_TILE):
        cols = pl.ds(n, IN_TILE)
        value = jnp.concatenate([high[b, own, :, cols].reshape(2 * FULL, IN_TILE) for b in range(3)], axis=0)
        taps_out[:, cols] = jnp.dot(wide_in[...], value, preferred_element_type=F32)
    for slot in (3, 0):
        passes[slot][0].wait_recv()
        shift_rows(slot, twin_others)

    for slot, late in ((0, late_0), (3, late_3)):
        for k in range(2):
            late[k].wait_recv()
            here = planes.at[slot, half(ch, k)]
            passes[slot].append(go(here, here, (sp, twin), planes.at[slot, half(twin, k)]))
        shift_rows(slot, mine)

    def outer(d):
        for n in range(0, CELLS, OUT_TILE):
            cols = pl.ds(n, OUT_TILE)
            value = high[:, 3 * d, :, cols].reshape(3 * FULL, OUT_TILE)
            taps_out[pl.ds(d * BAND, BAND), cols] += jnp.dot(wide_out[d], value, preferred_element_type=F32)

    rows = ROWS

    def slope(d, inside):
        def body(o, carry):
            at = pl.multiple_of(o * rows, rows)
            lane, column = lanes(rows)

            def tap(c):
                return taps_out[pl.ds(d * BAND + c * QUARTER + at, rows), :]

            pre = tap(1)
            pre = pre + jnp.where(column >= 1, roll(tap(0), 1), 0.0)
            pre = pre + jnp.where(column <= WIDTH - 2, roll(tap(2), -1), 0.0)
            s = 1.0 / (1.0 + jnp.exp(-pre))
            grad = cot[d, pl.ds(at, rows), :].astype(F32) * (s * (1.0 + pre * (1.0 - s)))
            grad = grad.astype(BF16)
            gedge[d, pl.ds(at, rows), :] = jnp.where(inside, grad, jnp.zeros_like(grad))
            shift_in(grad.astype(ROLL), at, rows, stacked, 1 + d)
            return carry

        lax.fori_loop(0, QUARTER // rows, body, 0)

    for landing in passes[0][1:]:
        landing.wait_recv()
    shift_rows(0, twins)
    outer(0)
    slope(0, sp > 0)
    g_down = go(gedge.at[0], ghalo.at[1], (down, ch), ghalo.at[1])
    for landing in passes[3][1:]:
        landing.wait_recv()
    shift_rows(3, twins)
    outer(1)
    slope(1, sp < 31)
    g_up = go(gedge.at[1], ghalo.at[0], (up, ch), ghalo.at[0])

    contract = (((1,), (1,)), ((), ()))

    def wgrad(a):
        total = None
        for d in range(2):
            term = lax.dot_general(
                stacked[pl.ds((1 + d) * STRIDE, STACK), :], planes[a + d], contract,
                preferred_element_type=F32,
            )
            total = term if total is None else total + term
        exact[pl.ds(a * 9, 9)] = total.reshape(9, QUARTER, FULL)
        part[pl.ds(a * 9, 9)] = total.astype(BF16).reshape(9, QUARTER, FULL)

    line_x = [(near(d, 0, 0), wrap(x + d, 4), wrap(x + 4 - d, 4)) for d in (2, 1, 3)]
    line_z = [(near(0, d, 0), wrap(z + d, 4), wrap(z + 4 - d, 4)) for d in (2, 1, 3)]
    halves = (
        dict(slot=0, cols=pl.ds(0, 128), me=x, line=line_x, owner=z, group=line_z, total=sum_x),
        dict(slot=1, cols=pl.ds(128, 128), me=z, line=line_z, owner=x, group=line_x, total=sum_z),
    )
    mate = (near(0, 0, 1), ch)

    def tile16(i):
        return pl.ds(pl.multiple_of(i * 16, 16), 16)

    def reduce_line(chunk):
        first, taps, per = chunk
        out = []
        for h in halves:
            for j, (peer, them, _) in enumerate(h["line"]):
                dst = got1.at[h["slot"], j, pl.ds(first, taps)]
                out.append(go(part.at[pl.ds(first, taps), tile16(them), h["cols"]], dst, (peer, ch), dst))
        return out

    def reduce_group(chunk, landings):
        first, taps, per = chunk
        out = []
        for h in halves:
            for landing in landings[3 * h["slot"] : 3 * h["slot"] + 3]:
                landing.wait_recv()
            total = exact[pl.ds(first, taps), tile16(h["me"]), h["cols"]]
            for j in range(3):
                total = total + got1[h["slot"], j, pl.ds(first, taps)].astype(F32)
            h["total"][pl.ds(first, taps)] = total
            if 4 * per > taps:
                h["total"][pl.ds(first + taps, 4 * per - taps)] = jnp.zeros((4 * per - taps, 16, 128), F32)
            for j, (peer, them, _) in enumerate(h["group"]):
                dst = got2.at[h["slot"], j, pl.ds(first // 4, per)]
                out.append(go(h["total"].at[pl.ds(first + them * per, per)], dst, (peer, ch), dst))
        return out

    def reduce_mate(chunk, landings):
        first, taps, per = chunk
        out = []
        for h in halves:
            for landing in landings[3 * h["slot"] : 3 * h["slot"] + 3]:
                landing.wait_recv()
            total = h["total"][pl.ds(first + h["owner"] * per, per)]
            for j in range(3):
                total = total + got2[h["slot"], j, pl.ds(first // 4, per)]
            here = (h["slot"], pl.ds(first // 4, per))
            middle[here] = total
            out.append(go(middle.at[here], got3.at[here], mate, got3.at[here]))
        return out

    def gather_group(chunk, landings):
        first, taps, per = chunk
        out = []
        for h in halves:
            landings[h["slot"]].wait_recv()
            here = (h["slot"], pl.ds(first // 4, per))
            total = middle[here] + got3[here]
            here = (pl.ds(first + h["owner"] * per, per), tile16(h["me"]), h["cols"])
            out_ref[here] = (total * SCALE).astype(BF16)
            for peer, _, from_them in h["group"]:
                lands = out_ref.at[pl.ds(first + from_them * per, per), tile16(h["me"]), h["cols"]]
                out.append(go(out_ref.at[here], out_ref.at[here], (peer, ch), lands))
        return out

    def gather_line(chunk, landings):
        first, taps, per = chunk
        out = []
        for h in halves:
            for landing in landings[3 * h["slot"] : 3 * h["slot"] + 3]:
                landing.wait_recv()
            here = out_ref.at[pl.ds(first, taps), tile16(h["me"]), h["cols"]]
            for peer, _, from_them in h["line"]:
                lands = out_ref.at[pl.ds(first, taps), tile16(from_them), h["cols"]]
                out.append(go(here, here, (peer, ch), lands))
        return out

    lines = []
    for a in range(3):
        wgrad(a)
        while len(lines) < len(CHUNKS) and sum(CHUNKS[len(lines)][:2]) <= 9 * a + 9:
            lines.append(reduce_line(CHUNKS[len(lines)]))

    for n in range(0, CELLS, D_TILE):
        cols = pl.ds(n, D_TILE)
        value = jnp.dot(
            turned_in[...].reshape(2 * FULL, 2 * STRIDE), stacked[pl.ds(STRIDE, 2 * STRIDE), cols],
            preferred_element_type=F32,
        )
        dx[:, :, cols] = value.reshape(2, FULL, D_TILE)

    def halo_shift(d):
        def body(o, carry):
            at = pl.multiple_of(o * rows, rows)
            shift_in(ghalo[d, pl.ds(at, rows), :].astype(ROLL), at, rows, stacked, 3 * d)
            return carry

        lax.fori_loop(0, QUARTER // rows, body, 0)

    def dgrad(d):
        for n in range(0, CELLS, D_TILE):
            cols = pl.ds(n, D_TILE)
            dx[d, :, cols] += jnp.dot(
                turned_out[d], stacked[pl.ds(3 * d * STRIDE, STRIDE), cols], preferred_element_type=F32
            )

    chips, crosses = [], []

    def neighbour(d, landing):
        landing.wait_recv()
        halo_shift(d)
        dgrad(d)
        dsend[d, 0] = dx[d, twins, :].astype(BF16)
        dsend[d, 1] = dx[d, twin_others, :].astype(BF16)
        chips.append((d, go(dsend.at[d], dgot.at[d], (sp, twin), dgot.at[d])))

    def cross_over(d, chip):
        chip.wait_recv()
        dsend2[d] = (dx[d, others, :] + dgot[d, 1].astype(F32)).astype(BF16)
        crosses.append((d, go(dsend2.at[d], dgot2.at[d], (sp, other), dgot2.at[d])))

    groups = [reduce_group(chunk, line) for chunk, line in zip(CHUNKS, lines)]
    n = len(CHUNKS)
    mates = [reduce_mate(CHUNKS[i], groups[i]) for i in range((n + 1) // 3)]
    neighbour(1, g_down)
    mates += [reduce_mate(CHUNKS[i], groups[i]) for i in range(len(mates), n - 1)]
    neighbour(0, g_up)
    mates += [reduce_mate(CHUNKS[i], groups[i]) for i in range(len(mates), n)]
    cross_over(*chips[0])
    broadcasts = [gather_group(CHUNKS[0], mates[0])]
    cross_over(*chips[1])
    broadcasts += [gather_group(chunk, mate_) for chunk, mate_ in zip(CHUNKS[1:], mates[1:])]
    finals = [gather_line(chunk, landings) for chunk, landings in zip(CHUNKS, broadcasts)]
    for d, cross in crosses:
        cross.wait_recv()
        gi_ref[d] = dx[d, mine, :] + dgot[d, 0].astype(F32) + dgot2[d].astype(F32)
    for landings in finals:
        for landing in landings:
            landing.wait_recv()
    for copy in sent:
        copy.wait_send()


COPIES = 7 + 4 + 8 + 2 + 2 + 2 + 26 * len(CHUNKS)


def local(features, weight, cotangent):
    vmem = pl.BlockSpec(memory_space=pltpu.VMEM)
    grad_input, grad_weight = pl.pallas_call(
        kernel,
        out_shape=(
            jax.ShapeDtypeStruct((2, QUARTER, CELLS), F32),
            jax.ShapeDtypeStruct((SLOTS, QUARTER, FULL), BF16),
        ),
        in_specs=[pl.BlockSpec(memory_space=pltpu.HBM)] * 3,
        out_specs=(vmem, vmem),
        scratch_shapes=[
            pltpu.VMEM((3, 4, FULL, CELLS), BF16),
            pltpu.VMEM((3, QUARTER, CELLS), BF16),
            pltpu.VMEM((2, QUARTER, CELLS), BF16),
            pltpu.VMEM((2 * BAND, 6 * FULL), BF16),
            pltpu.VMEM((2, BAND, 3 * FULL), BF16),
            pltpu.VMEM((2, FULL, 2 * STRIDE), BF16),
            pltpu.VMEM((2, FULL, STRIDE), BF16),
            pltpu.VMEM((2 * BAND, CELLS), F32),
            pltpu.VMEM((4 * STRIDE, CELLS), BF16),
            pltpu.VMEM((2, QUARTER, CELLS), BF16),
            pltpu.VMEM((2, QUARTER, CELLS), BF16),
            pltpu.VMEM((27, QUARTER, FULL), BF16),
            pltpu.VMEM((27, QUARTER, FULL), F32),
            pltpu.VMEM((SLOTS, 16, 128), F32),
            pltpu.VMEM((SLOTS, 16, 128), F32),
            pltpu.VMEM((2, 3, 27, 16, 128), BF16),
            pltpu.VMEM((2, 3, SLOTS // 4, 16, 128), F32),
            pltpu.VMEM((2, SLOTS // 4, 16, 128), F32),
            pltpu.VMEM((2, SLOTS // 4, 16, 128), F32),
            pltpu.VMEM((2, FULL, CELLS), F32),
            pltpu.VMEM((2, 2, QUARTER, CELLS), BF16),
            pltpu.VMEM((2, 2, QUARTER, CELLS), BF16),
            pltpu.VMEM((2, QUARTER, CELLS), BF16),
            pltpu.VMEM((2, QUARTER, CELLS), BF16),
            pltpu.SemaphoreType.DMA((20,)),
            pltpu.SemaphoreType.DMA((COPIES,)),
            pltpu.SemaphoreType.DMA((COPIES,)),
        ],
        compiler_params=pltpu.CompilerParams(
            collective_id=0, has_side_effects=True, vmem_limit_bytes=48 << 20
        ),
    )(*(pltpu.with_memory_space_constraint(v, pltpu.HBM) for v in (features, cotangent, weight.reshape(3, STACK, FULL))))
    return grad_input, grad_weight[:27].astype(F32)


def solution(mesh):
    placed = (P("sp", "ch", None), P(None, "ch", None), P("sp", "ch", None))
    return jax.shard_map(
        local,
        mesh=mesh,
        in_specs=placed,
        out_specs=(P("sp", "ch", None), P(None, "ch", None)),
        check_vma=False,
    )
```

```python
import functools

import jax
import jax.numpy as jnp
from jax import lax
from jax.experimental import pallas as pl
from jax.experimental.pallas import tpu as pltpu
from jax.sharding import PartitionSpec as P

MESH = pl.DeviceIdType.MESH
F32, BF16 = jnp.float32, jnp.bfloat16
WIDTH = 32
CELLS = 1024
QUARTER = 64
FULL = 256
STACK = 9 * QUARTER
BAND = 3 * QUARTER
TILE = 256
STRIDE = 640
IN_TILE, OUT_TILE, D_TILE, ROWS = 256, 256, 256, 64
ROLL = BF16
CHUNKS = ((0, 8, 2), (8, 8, 2), (16, 11, 3))
SLOTS = 28
SCALE = 1.0 / 256.0


def wrap(value, size):
    return lax.rem(value, size)


def place():
    sp, ch = lax.axis_index("sp"), lax.axis_index("ch")
    return sp, ch, lax.div(sp, 8), lax.rem(lax.div(sp, 2), 4), lax.rem(sp, 2)


def index(x, z, y):
    return x * 8 + z * 2 + y


def roll(value, shift):
    return pltpu.roll(value, shift % CELLS, 1)


def nine(value, lane, column):
    zero = jnp.zeros_like(value)
    wide = [
        jnp.where(column <= WIDTH - 2, roll(value, -1), zero),
        value,
        jnp.where(column >= 1, roll(value, 1), zero),
    ]
    out = [jnp.where(lane < CELLS - WIDTH, roll(v, -WIDTH), zero) for v in wide]
    out += wide
    out += [jnp.where(lane >= WIDTH, roll(v, WIDTH), zero) for v in wide]
    return out


def lanes(rows):
    lane = lax.broadcasted_iota(jnp.int32, (rows, CELLS), 1)
    return lane, lax.rem(lane, WIDTH)


def shift_in(value, row, rows, stacked, plane):
    lane, column = lanes(rows)
    for s, moved in enumerate(nine(value, lane, column)):
        stacked[pl.ds(plane * STRIDE + s * QUARTER + row, rows), :] = moved.astype(BF16)


def kernel(
    f_ref, cot_ref, w_ref, gi_ref, out_ref,
    high, edge, cot, wide_in, wide_out, turned_in, turned_out, taps_out, stacked, gedge, ghalo,
    part, exact, sum_x, sum_z, got1, got2, middle, got3, dx, dsend, dgot, dsend2, dgot2,
    local_sem, send_sem, recv_sem,
):
    planes = high.at[1]
    sp, ch, x, z, y = place()
    other = wrap(ch + 2, 4)
    twin = lax.div(ch, 2) * 2 + wrap(ch + 1, 2)
    twin_other = wrap(twin + 2, 4)
    up, down = wrap(sp + 1, 32), wrap(sp + 31, 32)

    def near(dx_, dz_, dy_):
        return index(wrap(x + dx_, 4), wrap(z + dz_, 4), wrap(y + dy_, 2))

    barrier = pltpu.get_barrier_semaphore()
    friends = [(sp, twin), (sp, other), (up, ch), (down, ch), (up, other), (down, other)]
    friends += [(near(d, 0, 0), ch) for d in (1, 2, 3)] + [(near(0, d, 0), ch) for d in (1, 2, 3)]
    friends.append((near(0, 0, 1), ch))
    for friend in friends:
        pl.semaphore_signal(barrier, inc=1, device_id=friend, device_id_type=MESH)

    own = pl.ds(1, 2)
    mine = pl.ds(pl.multiple_of(ch * QUARTER, QUARTER), QUARTER)
    others = pl.ds(pl.multiple_of(other * QUARTER, QUARTER), QUARTER)
    twins = pl.ds(pl.multiple_of(twin * QUARTER, QUARTER), QUARTER)
    twin_others = pl.ds(pl.multiple_of(twin_other * QUARTER, QUARTER), QUARTER)

    loads = [(f_ref, planes.at[own, mine]), (cot_ref, cot)]
    for b in range(3):
        rows_b = pl.ds(b * BAND, BAND)
        for d in range(2):
            for p in range(2):
                place_in = wide_in.at[pl.ds(d * BAND, BAND), pl.ds((2 * b + p) * FULL, FULL)]
                loads.append((w_ref.at[p + 1 - d, rows_b], place_in))
            loads.append((w_ref.at[2 * d, rows_b], wide_out.at[d, :, pl.ds(b * FULL, FULL)]))
    loads = [pltpu.make_async_copy(src, dst, local_sem.at[i]) for i, (src, dst) in enumerate(loads)]
    for load in loads:
        load.start()
    loads[0].wait()
    for e, plane, inside in ((0, 2, sp < 31), (1, 1, sp > 0)):
        value = planes[plane, mine, :]
        edge[e] = jnp.where(inside, value, jnp.zeros_like(value))

    def shift_rows(slot, rows):
        value = planes[slot, rows, :]
        lane, _ = lanes(QUARTER)
        zero = jnp.zeros_like(value)
        high[0, slot, rows, :] = jnp.where(lane >= WIDTH, roll(value, WIDTH), zero)
        high[2, slot, rows, :] = jnp.where(lane < CELLS - WIDTH, roll(value, -WIDTH), zero)

    pl.semaphore_wait(barrier, len(friends))

    sent = []

    def go(src, dst, device, lands):
        i = len(sent)

        def copy_to(ref):
            return pltpu.make_async_remote_copy(
                src_ref=src, dst_ref=ref, send_sem=send_sem.at[i], recv_sem=recv_sem.at[i],
                device_id=device, device_id_type=MESH,
            )

        copy = copy_to(dst)
        copy.start()
        sent.append(copy)
        return copy_to(lands)

    def cross_plane(slot):
        return go(planes.at[slot, mine], planes.at[slot, mine], (sp, other), planes.at[slot, others])

    def pass_plane(slot, rows, arriving):
        return go(planes.at[slot, rows], planes.at[slot, rows], (sp, twin), planes.at[slot, arriving])

    def halo(e, peer, slot):
        return go(edge.at[e], planes.at[slot, mine], (peer, other), planes.at[slot, others])

    across_2 = cross_plane(2)
    halo_3 = halo(1, down, 3)
    beside = go(planes.at[own, mine], planes.at[own, mine], (sp, twin), planes.at[own, twins])

    for load in loads[1:]:
        load.wait()
    for p in range(4):
        stacked[pl.ds(p * STRIDE + STACK, STRIDE - STACK), :] = jnp.zeros((STRIDE - STACK, CELLS), BF16)
    pad = jnp.zeros((FULL, STRIDE - STACK), BF16)
    for a, places in (
        (0, (turned_in.at[0, :, pl.ds(STRIDE, STRIDE)], turned_out.at[1])),
        (1, (turned_in.at[0, :, pl.ds(0, STRIDE)], turned_in.at[1, :, pl.ds(STRIDE, STRIDE)])),
        (2, (turned_in.at[1, :, pl.ds(0, STRIDE)], turned_out.at[0])),
    ):
        for s in range(9):
            b, rows_c = s // 3, pl.ds(s % 3 * QUARTER, QUARTER)
            if a == 1:
                block = wide_in[rows_c, pl.ds(2 * b * FULL, FULL)].T
            else:
                block = wide_out[a // 2, rows_c, pl.ds(b * FULL, FULL)].T
            for dst in places:
                dst[:, pl.ds(s * QUARTER, QUARTER)] = block
        for dst in places:
            dst[:, pl.ds(STACK, STRIDE - STACK)] = pad
    across_1 = cross_plane(1)
    halo_0 = halo(0, up, 0)
    for slot in (1, 2):
        shift_rows(slot, mine)

    across_2.wait_recv()
    value = planes[2, others, :]
    edge[2] = jnp.where(sp < 31, value, jnp.zeros_like(value))
    late_0 = go(edge.at[2], planes.at[0, others], (up, other), planes.at[0, mine])
    passed = [pass_plane(2, others, twin_others)]
    halo_3.wait_recv()
    late_3 = go(planes.at[3, others], planes.at[3, others], (sp, other), planes.at[3, mine])
    across_1.wait_recv()
    passed.append(pass_plane(1, others, twin_others))
    passes = {3: [pass_plane(3, others, twin_others)]}
    halo_0.wait_recv()
    passes[0] = [pass_plane(0, others, twin_others)]
    for slot in (2, 1, 3, 0):
        shift_rows(slot, others)
    beside.wait_recv()
    for slot in (1, 2):
        shift_rows(slot, twins)
    for slot, landing in zip((2, 1), passed):
        landing.wait_recv()
        shift_rows(slot, twin_others)

    for n in range(0, CELLS, IN_TILE):
        cols = pl.ds(n, IN_TILE)
        value = jnp.concatenate([high[b, own, :, cols].reshape(2 * FULL, IN_TILE) for b in range(3)], axis=0)
        taps_out[:, cols] = jnp.dot(wide_in[...], value, preferred_element_type=F32)
    for slot in (3, 0):
        passes[slot][0].wait_recv()
        shift_rows(slot, twin_others)

    for slot, late in ((0, late_0), (3, late_3)):
        late.wait_recv()
        passes[slot].append(pass_plane(slot, mine, twins))
        shift_rows(slot, mine)

    def outer(d):
        for n in range(0, CELLS, OUT_TILE):
            cols = pl.ds(n, OUT_TILE)
            value = high[:, 3 * d, :, cols].reshape(3 * FULL, OUT_TILE)
            taps_out[pl.ds(d * BAND, BAND), cols] += jnp.dot(wide_out[d], value, preferred_element_type=F32)

    rows = ROWS

    def slope(d, inside):
        def body(o, carry):
            at = pl.multiple_of(o * rows, rows)
            lane, column = lanes(rows)

            def tap(c):
                return taps_out[pl.ds(d * BAND + c * QUARTER + at, rows), :]

            pre = tap(1)
            pre = pre + jnp.where(column >= 1, roll(tap(0), 1), 0.0)
            pre = pre + jnp.where(column <= WIDTH - 2, roll(tap(2), -1), 0.0)
            s = 1.0 / (1.0 + jnp.exp(-pre))
            grad = cot[d, pl.ds(at, rows), :].astype(F32) * (s * (1.0 + pre * (1.0 - s)))
            grad = grad.astype(BF16)
            gedge[d, pl.ds(at, rows), :] = jnp.where(inside, grad, jnp.zeros_like(grad))
            shift_in(grad.astype(ROLL), at, rows, stacked, 1 + d)
            return carry

        lax.fori_loop(0, QUARTER // rows, body, 0)

    passes[0][1].wait_recv()
    shift_rows(0, twins)
    outer(0)
    slope(0, sp > 0)
    g_down = go(gedge.at[0], ghalo.at[1], (down, ch), ghalo.at[1])
    passes[3][1].wait_recv()
    shift_rows(3, twins)
    outer(1)
    slope(1, sp < 31)
    g_up = go(gedge.at[1], ghalo.at[0], (up, ch), ghalo.at[0])

    contract = (((1,), (1,)), ((), ()))

    def wgrad(a):
        total = None
        for d in range(2):
            term = lax.dot_general(
                stacked[pl.ds((1 + d) * STRIDE, STACK), :], planes[a + d], contract,
                preferred_element_type=F32,
            )
            total = term if total is None else total + term
        exact[pl.ds(a * 9, 9)] = total.reshape(9, QUARTER, FULL)
        part[pl.ds(a * 9, 9)] = total.astype(BF16).reshape(9, QUARTER, FULL)

    line_x = [(near(d, 0, 0), wrap(x + d, 4), wrap(x + 4 - d, 4)) for d in (2, 1, 3)]
    line_z = [(near(0, d, 0), wrap(z + d, 4), wrap(z + 4 - d, 4)) for d in (2, 1, 3)]
    halves = (
        dict(slot=0, cols=pl.ds(0, 128), me=x, line=line_x, owner=z, group=line_z, total=sum_x),
        dict(slot=1, cols=pl.ds(128, 128), me=z, line=line_z, owner=x, group=line_x, total=sum_z),
    )
    mate = (near(0, 0, 1), ch)

    def tile16(i):
        return pl.ds(pl.multiple_of(i * 16, 16), 16)

    def reduce_line(chunk):
        first, taps, per = chunk
        out = []
        for h in halves:
            for j, (peer, them, _) in enumerate(h["line"]):
                dst = got1.at[h["slot"], j, pl.ds(first, taps)]
                out.append(go(part.at[pl.ds(first, taps), tile16(them), h["cols"]], dst, (peer, ch), dst))
        return out

    def reduce_group(chunk, landings):
        first, taps, per = chunk
        out = []
        for h in halves:
            for landing in landings[3 * h["slot"] : 3 * h["slot"] + 3]:
                landing.wait_recv()
            total = exact[pl.ds(first, taps), tile16(h["me"]), h["cols"]]
            for j in range(3):
                total = total + got1[h["slot"], j, pl.ds(first, taps)].astype(F32)
            h["total"][pl.ds(first, taps)] = total
            if 4 * per > taps:
                h["total"][pl.ds(first + taps, 4 * per - taps)] = jnp.zeros((4 * per - taps, 16, 128), F32)
            for j, (peer, them, _) in enumerate(h["group"]):
                dst = got2.at[h["slot"], j, pl.ds(first // 4, per)]
                out.append(go(h["total"].at[pl.ds(first + them * per, per)], dst, (peer, ch), dst))
        return out

    def reduce_mate(chunk, landings):
        first, taps, per = chunk
        out = []
        for h in halves:
            for landing in landings[3 * h["slot"] : 3 * h["slot"] + 3]:
                landing.wait_recv()
            total = h["total"][pl.ds(first + h["owner"] * per, per)]
            for j in range(3):
                total = total + got2[h["slot"], j, pl.ds(first // 4, per)]
            here = (h["slot"], pl.ds(first // 4, per))
            middle[here] = total
            out.append(go(middle.at[here], got3.at[here], mate, got3.at[here]))
        return out

    def gather_group(chunk, landings):
        first, taps, per = chunk
        out = []
        for h in halves:
            landings[h["slot"]].wait_recv()
            here = (h["slot"], pl.ds(first // 4, per))
            total = middle[here] + got3[here]
            here = (pl.ds(first + h["owner"] * per, per), tile16(h["me"]), h["cols"])
            out_ref[here] = (total * SCALE).astype(BF16)
            for peer, _, from_them in h["group"]:
                lands = out_ref.at[pl.ds(first + from_them * per, per), tile16(h["me"]), h["cols"]]
                out.append(go(out_ref.at[here], out_ref.at[here], (peer, ch), lands))
        return out

    def gather_line(chunk, landings):
        first, taps, per = chunk
        out = []
        for h in halves:
            for landing in landings[3 * h["slot"] : 3 * h["slot"] + 3]:
                landing.wait_recv()
            here = out_ref.at[pl.ds(first, taps), tile16(h["me"]), h["cols"]]
            for peer, _, from_them in h["line"]:
                lands = out_ref.at[pl.ds(first, taps), tile16(from_them), h["cols"]]
                out.append(go(here, here, (peer, ch), lands))
        return out

    lines = []
    for a in range(3):
        wgrad(a)
        while len(lines) < len(CHUNKS) and sum(CHUNKS[len(lines)][:2]) <= 9 * a + 9:
            lines.append(reduce_line(CHUNKS[len(lines)]))

    for n in range(0, CELLS, D_TILE):
        cols = pl.ds(n, D_TILE)
        value = jnp.dot(
            turned_in[...].reshape(2 * FULL, 2 * STRIDE), stacked[pl.ds(STRIDE, 2 * STRIDE), cols],
            preferred_element_type=F32,
        )
        dx[:, :, cols] = value.reshape(2, FULL, D_TILE)

    def halo_shift(d):
        def body(o, carry):
            at = pl.multiple_of(o * rows, rows)
            shift_in(ghalo[d, pl.ds(at, rows), :].astype(ROLL), at, rows, stacked, 3 * d)
            return carry

        lax.fori_loop(0, QUARTER // rows, body, 0)

    def dgrad(d):
        for n in range(0, CELLS, D_TILE):
            cols = pl.ds(n, D_TILE)
            dx[d, :, cols] += jnp.dot(
                turned_out[d], stacked[pl.ds(3 * d * STRIDE, STRIDE), cols], preferred_element_type=F32
            )

    chips, crosses = [], []

    def neighbour(d, landing):
        landing.wait_recv()
        halo_shift(d)
        dgrad(d)
        dsend[d, 0] = dx[d, twins, :].astype(BF16)
        dsend[d, 1] = dx[d, twin_others, :].astype(BF16)
        chips.append((d, go(dsend.at[d], dgot.at[d], (sp, twin), dgot.at[d])))

    def cross_over(d, chip):
        chip.wait_recv()
        dsend2[d] = (dx[d, others, :] + dgot[d, 1].astype(F32)).astype(BF16)
        crosses.append((d, go(dsend2.at[d], dgot2.at[d], (sp, other), dgot2.at[d])))

    groups = [reduce_group(chunk, line) for chunk, line in zip(CHUNKS, lines)]
    n = len(CHUNKS)
    mates = [reduce_mate(CHUNKS[i], groups[i]) for i in range((n + 1) // 3)]
    neighbour(1, g_down)
    mates += [reduce_mate(CHUNKS[i], groups[i]) for i in range(len(mates), n - 1)]
    neighbour(0, g_up)
    mates += [reduce_mate(CHUNKS[i], groups[i]) for i in range(len(mates), n)]
    cross_over(*chips[0])
    broadcasts = [gather_group(CHUNKS[0], mates[0])]
    cross_over(*chips[1])
    broadcasts += [gather_group(chunk, mate_) for chunk, mate_ in zip(CHUNKS[1:], mates[1:])]
    finals = [gather_line(chunk, landings) for chunk, landings in zip(CHUNKS, broadcasts)]
    for d, cross in crosses:
        cross.wait_recv()
        gi_ref[d] = dx[d, mine, :] + dgot[d, 0].astype(F32) + dgot2[d].astype(F32)
    for landings in finals:
        for landing in landings:
            landing.wait_recv()
    for copy in sent:
        copy.wait_send()


COPIES = 5 + 2 + 6 + 2 + 2 + 2 + 26 * len(CHUNKS)


def local(features, weight, cotangent):
    vmem = pl.BlockSpec(memory_space=pltpu.VMEM)
    grad_input, grad_weight = pl.pallas_call(
        kernel,
        out_shape=(
            jax.ShapeDtypeStruct((2, QUARTER, CELLS), F32),
            jax.ShapeDtypeStruct((SLOTS, QUARTER, FULL), BF16),
        ),
        in_specs=[pl.BlockSpec(memory_space=pltpu.HBM)] * 3,
        out_specs=(vmem, vmem),
        scratch_shapes=[
            pltpu.VMEM((3, 4, FULL, CELLS), BF16),
            pltpu.VMEM((3, QUARTER, CELLS), BF16),
            pltpu.VMEM((2, QUARTER, CELLS), BF16),
            pltpu.VMEM((2 * BAND, 6 * FULL), BF16),
            pltpu.VMEM((2, BAND, 3 * FULL), BF16),
            pltpu.VMEM((2, FULL, 2 * STRIDE), BF16),
            pltpu.VMEM((2, FULL, STRIDE), BF16),
            pltpu.VMEM((2 * BAND, CELLS), F32),
            pltpu.VMEM((4 * STRIDE, CELLS), BF16),
            pltpu.VMEM((2, QUARTER, CELLS), BF16),
            pltpu.VMEM((2, QUARTER, CELLS), BF16),
            pltpu.VMEM((27, QUARTER, FULL), BF16),
            pltpu.VMEM((27, QUARTER, FULL), F32),
            pltpu.VMEM((SLOTS, 16, 128), F32),
            pltpu.VMEM((SLOTS, 16, 128), F32),
            pltpu.VMEM((2, 3, 27, 16, 128), BF16),
            pltpu.VMEM((2, 3, SLOTS // 4, 16, 128), F32),
            pltpu.VMEM((2, SLOTS // 4, 16, 128), F32),
            pltpu.VMEM((2, SLOTS // 4, 16, 128), F32),
            pltpu.VMEM((2, FULL, CELLS), F32),
            pltpu.VMEM((2, 2, QUARTER, CELLS), BF16),
            pltpu.VMEM((2, 2, QUARTER, CELLS), BF16),
            pltpu.VMEM((2, QUARTER, CELLS), BF16),
            pltpu.VMEM((2, QUARTER, CELLS), BF16),
            pltpu.SemaphoreType.DMA((20,)),
            pltpu.SemaphoreType.DMA((COPIES,)),
            pltpu.SemaphoreType.DMA((COPIES,)),
        ],
        compiler_params=pltpu.CompilerParams(
            collective_id=0, has_side_effects=True, vmem_limit_bytes=48 << 20
        ),
    )(*(pltpu.with_memory_space_constraint(v, pltpu.HBM) for v in (features, cotangent, weight.reshape(3, STACK, FULL))))
    return grad_input, grad_weight[:27].astype(F32)


def solution(mesh):
    placed = (P("sp", "ch", None), P(None, "ch", None), P("sp", "ch", None))
    return jax.shard_map(
        local,
        mesh=mesh,
        in_specs=placed,
        out_specs=(P("sp", "ch", None), P(None, "ch", None)),
        check_vma=False,
    )
```

```python
import functools

import jax
import jax.numpy as jnp
from jax import lax
from jax.experimental import pallas as pl
from jax.experimental.pallas import tpu as pltpu
from jax.sharding import PartitionSpec as P

MESH = pl.DeviceIdType.MESH
F32, BF16 = jnp.float32, jnp.bfloat16
WIDTH = 32
CELLS = 1024
QUARTER = 64
FULL = 256
STACK = 9 * QUARTER
BAND = 3 * QUARTER
TILE = 256
STRIDE = 640
IN_TILE, OUT_TILE, D_TILE, ROWS = 512, 512, 512, 64
ROLL = BF16
CHUNKS = ((0, 8, 2), (8, 8, 2), (16, 11, 3))
SLOTS = 28
SCALE = 1.0 / 256.0


def wrap(value, size):
    return lax.rem(value, size)


def place():
    sp, ch = lax.axis_index("sp"), lax.axis_index("ch")
    return sp, ch, lax.div(sp, 8), lax.rem(lax.div(sp, 2), 4), lax.rem(sp, 2)


def index(x, z, y):
    return x * 8 + z * 2 + y


def roll(value, shift):
    return pltpu.roll(value, shift % CELLS, 1)


def nine(value, lane, column):
    zero = jnp.zeros_like(value)
    wide = [
        jnp.where(column <= WIDTH - 2, roll(value, -1), zero),
        value,
        jnp.where(column >= 1, roll(value, 1), zero),
    ]
    out = [jnp.where(lane < CELLS - WIDTH, roll(v, -WIDTH), zero) for v in wide]
    out += wide
    out += [jnp.where(lane >= WIDTH, roll(v, WIDTH), zero) for v in wide]
    return out


def lanes(rows):
    lane = lax.broadcasted_iota(jnp.int32, (rows, CELLS), 1)
    return lane, lax.rem(lane, WIDTH)


def shift_in(value, row, rows, stacked, plane):
    lane, column = lanes(rows)
    for s, moved in enumerate(nine(value, lane, column)):
        stacked[pl.ds(plane * STRIDE + s * QUARTER + row, rows), :] = moved.astype(BF16)


def kernel(
    f_ref, cot_ref, w_ref, gi_ref, out_ref,
    high, edge, cot, wide_in, wide_out, turned_in, turned_out, taps_out, stacked, gedge, ghalo,
    part, exact, sum_x, sum_z, got1, got2, middle, got3, dx, dsend, dgot, dsend2, dgot2,
    local_sem, send_sem, recv_sem,
):
    planes = high.at[1]
    sp, ch, x, z, y = place()
    other = wrap(ch + 2, 4)
    twin = lax.div(ch, 2) * 2 + wrap(ch + 1, 2)
    twin_other = wrap(twin + 2, 4)
    up, down = wrap(sp + 1, 32), wrap(sp + 31, 32)

    def near(dx_, dz_, dy_):
        return index(wrap(x + dx_, 4), wrap(z + dz_, 4), wrap(y + dy_, 2))

    barrier = pltpu.get_barrier_semaphore()
    friends = [(sp, twin), (sp, other), (up, ch), (down, ch), (up, other), (down, other)]
    friends += [(near(d, 0, 0), ch) for d in (1, 2, 3)] + [(near(0, d, 0), ch) for d in (1, 2, 3)]
    friends.append((near(0, 0, 1), ch))
    for friend in friends:
        pl.semaphore_signal(barrier, inc=1, device_id=friend, device_id_type=MESH)

    own = pl.ds(1, 2)
    mine = pl.ds(pl.multiple_of(ch * QUARTER, QUARTER), QUARTER)
    others = pl.ds(pl.multiple_of(other * QUARTER, QUARTER), QUARTER)
    twins = pl.ds(pl.multiple_of(twin * QUARTER, QUARTER), QUARTER)
    twin_others = pl.ds(pl.multiple_of(twin_other * QUARTER, QUARTER), QUARTER)

    loads = [(f_ref, planes.at[own, mine]), (cot_ref, cot)]
    for b in range(3):
        rows_b = pl.ds(b * BAND, BAND)
        for d in range(2):
            for p in range(2):
                place_in = wide_in.at[pl.ds(d * BAND, BAND), pl.ds((2 * b + p) * FULL, FULL)]
                loads.append((w_ref.at[p + 1 - d, rows_b], place_in))
            loads.append((w_ref.at[2 * d, rows_b], wide_out.at[d, :, pl.ds(b * FULL, FULL)]))
    loads = [pltpu.make_async_copy(src, dst, local_sem.at[i]) for i, (src, dst) in enumerate(loads)]
    for load in loads:
        load.start()
    loads[0].wait()
    for e, plane, inside in ((0, 2, sp < 31), (1, 1, sp > 0)):
        value = planes[plane, mine, :]
        edge[e] = jnp.where(inside, value, jnp.zeros_like(value))

    def shift_rows(slot, rows):
        value = planes[slot, rows, :]
        lane, _ = lanes(QUARTER)
        zero = jnp.zeros_like(value)
        high[0, slot, rows, :] = jnp.where(lane >= WIDTH, roll(value, WIDTH), zero)
        high[2, slot, rows, :] = jnp.where(lane < CELLS - WIDTH, roll(value, -WIDTH), zero)

    pl.semaphore_wait(barrier, len(friends))

    sent = []

    def go(src, dst, device, lands):
        i = len(sent)

        def copy_to(ref):
            return pltpu.make_async_remote_copy(
                src_ref=src, dst_ref=ref, send_sem=send_sem.at[i], recv_sem=recv_sem.at[i],
                device_id=device, device_id_type=MESH,
            )

        copy = copy_to(dst)
        copy.start()
        sent.append(copy)
        return copy_to(lands)

    def cross_plane(slot):
        return go(planes.at[slot, mine], planes.at[slot, mine], (sp, other), planes.at[slot, others])

    def pass_plane(slot, rows, arriving):
        return go(planes.at[slot, rows], planes.at[slot, rows], (sp, twin), planes.at[slot, arriving])

    def halo(e, peer, slot):
        return go(edge.at[e], planes.at[slot, mine], (peer, other), planes.at[slot, others])

    across_2 = cross_plane(2)
    halo_3 = halo(1, down, 3)
    across_1 = cross_plane(1)
    halo_0 = halo(0, up, 0)
    beside = go(planes.at[own, mine], planes.at[own, mine], (sp, twin), planes.at[own, twins])

    for load in loads[1:]:
        load.wait()
    for p in range(4):
        stacked[pl.ds(p * STRIDE + STACK, STRIDE - STACK), :] = jnp.zeros((STRIDE - STACK, CELLS), BF16)
    pad = jnp.zeros((FULL, STRIDE - STACK), BF16)
    for a, places in (
        (0, (turned_in.at[0, :, pl.ds(STRIDE, STRIDE)], turned_out.at[1])),
        (1, (turned_in.at[0, :, pl.ds(0, STRIDE)], turned_in.at[1, :, pl.ds(STRIDE, STRIDE)])),
        (2, (turned_in.at[1, :, pl.ds(0, STRIDE)], turned_out.at[0])),
    ):
        for s in range(9):
            b, rows_c = s // 3, pl.ds(s % 3 * QUARTER, QUARTER)
            if a == 1:
                block = wide_in[rows_c, pl.ds(2 * b * FULL, FULL)].T
            else:
                block = wide_out[a // 2, rows_c, pl.ds(b * FULL, FULL)].T
            for dst in places:
                dst[:, pl.ds(s * QUARTER, QUARTER)] = block
        for dst in places:
            dst[:, pl.ds(STACK, STRIDE - STACK)] = pad
    for slot in (1, 2):
        shift_rows(slot, mine)

    across_2.wait_recv()
    value = planes[2, others, :]
    edge[2] = jnp.where(sp < 31, value, jnp.zeros_like(value))
    late_0 = go(edge.at[2], planes.at[0, others], (up, other), planes.at[0, mine])
    passed = [pass_plane(2, others, twin_others)]
    halo_3.wait_recv()
    late_3 = go(planes.at[3, others], planes.at[3, others], (sp, other), planes.at[3, mine])
    across_1.wait_recv()
    passed.append(pass_plane(1, others, twin_others))
    passes = {3: [pass_plane(3, others, twin_others)]}
    halo_0.wait_recv()
    passes[0] = [pass_plane(0, others, twin_others)]
    for slot in (2, 1, 3, 0):
        shift_rows(slot, others)
    beside.wait_recv()
    for slot in (1, 2):
        shift_rows(slot, twins)
    for slot, landing in zip((2, 1), passed):
        landing.wait_recv()
        shift_rows(slot, twin_others)

    for n in range(0, CELLS, IN_TILE):
        cols = pl.ds(n, IN_TILE)
        value = jnp.concatenate([high[b, own, :, cols].reshape(2 * FULL, IN_TILE) for b in range(3)], axis=0)
        taps_out[:, cols] = jnp.dot(wide_in[...], value, preferred_element_type=F32)
    for slot in (3, 0):
        passes[slot][0].wait_recv()
        shift_rows(slot, twin_others)

    for slot, late in ((0, late_0), (3, late_3)):
        late.wait_recv()
        passes[slot].append(pass_plane(slot, mine, twins))
        shift_rows(slot, mine)

    def outer(d):
        for n in range(0, CELLS, OUT_TILE):
            cols = pl.ds(n, OUT_TILE)
            value = high[:, 3 * d, :, cols].reshape(3 * FULL, OUT_TILE)
            taps_out[pl.ds(d * BAND, BAND), cols] += jnp.dot(wide_out[d], value, preferred_element_type=F32)

    rows = ROWS

    def slope(d, inside):
        def body(o, carry):
            at = pl.multiple_of(o * rows, rows)
            lane, column = lanes(rows)

            def tap(c):
                return taps_out[pl.ds(d * BAND + c * QUARTER + at, rows), :]

            pre = tap(1)
            pre = pre + jnp.where(column >= 1, roll(tap(0), 1), 0.0)
            pre = pre + jnp.where(column <= WIDTH - 2, roll(tap(2), -1), 0.0)
            s = 1.0 / (1.0 + jnp.exp(-pre))
            grad = cot[d, pl.ds(at, rows), :].astype(F32) * (s * (1.0 + pre * (1.0 - s)))
            grad = grad.astype(BF16)
            gedge[d, pl.ds(at, rows), :] = jnp.where(inside, grad, jnp.zeros_like(grad))
            shift_in(grad.astype(ROLL), at, rows, stacked, 1 + d)
            return carry

        lax.fori_loop(0, QUARTER // rows, body, 0)

    passes[0][1].wait_recv()
    shift_rows(0, twins)
    outer(0)
    slope(0, sp > 0)
    g_down = go(gedge.at[0], ghalo.at[1], (down, ch), ghalo.at[1])
    passes[3][1].wait_recv()
    shift_rows(3, twins)
    outer(1)
    slope(1, sp < 31)
    g_up = go(gedge.at[1], ghalo.at[0], (up, ch), ghalo.at[0])

    contract = (((1,), (1,)), ((), ()))

    def wgrad(a):
        total = None
        for d in range(2):
            term = lax.dot_general(
                stacked[pl.ds((1 + d) * STRIDE, STACK), :], planes[a + d], contract,
                preferred_element_type=F32,
            )
            total = term if total is None else total + term
        exact[pl.ds(a * 9, 9)] = total.reshape(9, QUARTER, FULL)
        part[pl.ds(a * 9, 9)] = total.astype(BF16).reshape(9, QUARTER, FULL)

    line_x = [(near(d, 0, 0), wrap(x + d, 4), wrap(x + 4 - d, 4)) for d in (2, 1, 3)]
    line_z = [(near(0, d, 0), wrap(z + d, 4), wrap(z + 4 - d, 4)) for d in (2, 1, 3)]
    halves = (
        dict(slot=0, cols=pl.ds(0, 128), me=x, line=line_x, owner=z, group=line_z, total=sum_x),
        dict(slot=1, cols=pl.ds(128, 128), me=z, line=line_z, owner=x, group=line_x, total=sum_z),
    )
    mate = (near(0, 0, 1), ch)

    def tile16(i):
        return pl.ds(pl.multiple_of(i * 16, 16), 16)

    def reduce_line(chunk):
        first, taps, per = chunk
        out = []
        for h in halves:
            for j, (peer, them, _) in enumerate(h["line"]):
                dst = got1.at[h["slot"], j, pl.ds(first, taps)]
                out.append(go(part.at[pl.ds(first, taps), tile16(them), h["cols"]], dst, (peer, ch), dst))
        return out

    def reduce_group(chunk, landings):
        first, taps, per = chunk
        out = []
        for h in halves:
            for landing in landings[3 * h["slot"] : 3 * h["slot"] + 3]:
                landing.wait_recv()
            total = exact[pl.ds(first, taps), tile16(h["me"]), h["cols"]]
            for j in range(3):
                total = total + got1[h["slot"], j, pl.ds(first, taps)].astype(F32)
            h["total"][pl.ds(first, taps)] = total
            if 4 * per > taps:
                h["total"][pl.ds(first + taps, 4 * per - taps)] = jnp.zeros((4 * per - taps, 16, 128), F32)
            for j, (peer, them, _) in enumerate(h["group"]):
                dst = got2.at[h["slot"], j, pl.ds(first // 4, per)]
                out.append(go(h["total"].at[pl.ds(first + them * per, per)], dst, (peer, ch), dst))
        return out

    def reduce_mate(chunk, landings):
        first, taps, per = chunk
        out = []
        for h in halves:
            for landing in landings[3 * h["slot"] : 3 * h["slot"] + 3]:
                landing.wait_recv()
            total = h["total"][pl.ds(first + h["owner"] * per, per)]
            for j in range(3):
                total = total + got2[h["slot"], j, pl.ds(first // 4, per)]
            here = (h["slot"], pl.ds(first // 4, per))
            middle[here] = total
            out.append(go(middle.at[here], got3.at[here], mate, got3.at[here]))
        return out

    def gather_group(chunk, landings):
        first, taps, per = chunk
        out = []
        for h in halves:
            landings[h["slot"]].wait_recv()
            here = (h["slot"], pl.ds(first // 4, per))
            total = middle[here] + got3[here]
            here = (pl.ds(first + h["owner"] * per, per), tile16(h["me"]), h["cols"])
            out_ref[here] = (total * SCALE).astype(BF16)
            for peer, _, from_them in h["group"]:
                lands = out_ref.at[pl.ds(first + from_them * per, per), tile16(h["me"]), h["cols"]]
                out.append(go(out_ref.at[here], out_ref.at[here], (peer, ch), lands))
        return out

    def gather_line(chunk, landings):
        first, taps, per = chunk
        out = []
        for h in halves:
            for landing in landings[3 * h["slot"] : 3 * h["slot"] + 3]:
                landing.wait_recv()
            here = out_ref.at[pl.ds(first, taps), tile16(h["me"]), h["cols"]]
            for peer, _, from_them in h["line"]:
                lands = out_ref.at[pl.ds(first, taps), tile16(from_them), h["cols"]]
                out.append(go(here, here, (peer, ch), lands))
        return out

    lines = []
    for a in range(3):
        wgrad(a)
        while len(lines) < len(CHUNKS) and sum(CHUNKS[len(lines)][:2]) <= 9 * a + 9:
            lines.append(reduce_line(CHUNKS[len(lines)]))

    for n in range(0, CELLS, D_TILE):
        cols = pl.ds(n, D_TILE)
        value = jnp.dot(
            turned_in[...].reshape(2 * FULL, 2 * STRIDE), stacked[pl.ds(STRIDE, 2 * STRIDE), cols],
            preferred_element_type=F32,
        )
        dx[:, :, cols] = value.reshape(2, FULL, D_TILE)

    def halo_shift(d):
        def body(o, carry):
            at = pl.multiple_of(o * rows, rows)
            shift_in(ghalo[d, pl.ds(at, rows), :].astype(ROLL), at, rows, stacked, 3 * d)
            return carry

        lax.fori_loop(0, QUARTER // rows, body, 0)

    def dgrad(d):
        for n in range(0, CELLS, D_TILE):
            cols = pl.ds(n, D_TILE)
            dx[d, :, cols] += jnp.dot(
                turned_out[d], stacked[pl.ds(3 * d * STRIDE, STRIDE), cols], preferred_element_type=F32
            )

    chips, crosses = [], []

    def neighbour(d, landing):
        landing.wait_recv()
        halo_shift(d)
        dgrad(d)
        dsend[d, 0] = dx[d, twins, :].astype(BF16)
        dsend[d, 1] = dx[d, twin_others, :].astype(BF16)
        chips.append((d, go(dsend.at[d], dgot.at[d], (sp, twin), dgot.at[d])))

    def cross_over(d, chip):
        chip.wait_recv()
        dsend2[d] = (dx[d, others, :] + dgot[d, 1].astype(F32)).astype(BF16)
        crosses.append((d, go(dsend2.at[d], dgot2.at[d], (sp, other), dgot2.at[d])))

    groups = [reduce_group(chunk, line) for chunk, line in zip(CHUNKS, lines)]
    n = len(CHUNKS)
    mates = [reduce_mate(CHUNKS[i], groups[i]) for i in range((n + 1) // 3)]
    neighbour(1, g_down)
    mates += [reduce_mate(CHUNKS[i], groups[i]) for i in range(len(mates), n - 1)]
    neighbour(0, g_up)
    mates += [reduce_mate(CHUNKS[i], groups[i]) for i in range(len(mates), n)]
    cross_over(*chips[0])
    broadcasts = [gather_group(CHUNKS[0], mates[0])]
    cross_over(*chips[1])
    broadcasts += [gather_group(chunk, mate_) for chunk, mate_ in zip(CHUNKS[1:], mates[1:])]
    finals = [gather_line(chunk, landings) for chunk, landings in zip(CHUNKS, broadcasts)]
    for d, cross in crosses:
        cross.wait_recv()
        gi_ref[d] = dx[d, mine, :] + dgot[d, 0].astype(F32) + dgot2[d].astype(F32)
    for landings in finals:
        for landing in landings:
            landing.wait_recv()
    for copy in sent:
        copy.wait_send()


COPIES = 5 + 2 + 6 + 2 + 2 + 2 + 26 * len(CHUNKS)


def local(features, weight, cotangent):
    vmem = pl.BlockSpec(memory_space=pltpu.VMEM)
    grad_input, grad_weight = pl.pallas_call(
        kernel,
        out_shape=(
            jax.ShapeDtypeStruct((2, QUARTER, CELLS), F32),
            jax.ShapeDtypeStruct((SLOTS, QUARTER, FULL), BF16),
        ),
        in_specs=[pl.BlockSpec(memory_space=pltpu.HBM)] * 3,
        out_specs=(vmem, vmem),
        scratch_shapes=[
            pltpu.VMEM((3, 4, FULL, CELLS), BF16),
            pltpu.VMEM((3, QUARTER, CELLS), BF16),
            pltpu.VMEM((2, QUARTER, CELLS), BF16),
            pltpu.VMEM((2 * BAND, 6 * FULL), BF16),
            pltpu.VMEM((2, BAND, 3 * FULL), BF16),
            pltpu.VMEM((2, FULL, 2 * STRIDE), BF16),
            pltpu.VMEM((2, FULL, STRIDE), BF16),
            pltpu.VMEM((2 * BAND, CELLS), F32),
            pltpu.VMEM((4 * STRIDE, CELLS), BF16),
            pltpu.VMEM((2, QUARTER, CELLS), BF16),
            pltpu.VMEM((2, QUARTER, CELLS), BF16),
            pltpu.VMEM((27, QUARTER, FULL), BF16),
            pltpu.VMEM((27, QUARTER, FULL), F32),
            pltpu.VMEM((SLOTS, 16, 128), F32),
            pltpu.VMEM((SLOTS, 16, 128), F32),
            pltpu.VMEM((2, 3, 27, 16, 128), BF16),
            pltpu.VMEM((2, 3, SLOTS // 4, 16, 128), F32),
            pltpu.VMEM((2, SLOTS // 4, 16, 128), F32),
            pltpu.VMEM((2, SLOTS // 4, 16, 128), F32),
            pltpu.VMEM((2, FULL, CELLS), F32),
            pltpu.VMEM((2, 2, QUARTER, CELLS), BF16),
            pltpu.VMEM((2, 2, QUARTER, CELLS), BF16),
            pltpu.VMEM((2, QUARTER, CELLS), BF16),
            pltpu.VMEM((2, QUARTER, CELLS), BF16),
            pltpu.SemaphoreType.DMA((20,)),
            pltpu.SemaphoreType.DMA((COPIES,)),
            pltpu.SemaphoreType.DMA((COPIES,)),
        ],
        compiler_params=pltpu.CompilerParams(
            collective_id=0, has_side_effects=True, vmem_limit_bytes=48 << 20
        ),
    )(*(pltpu.with_memory_space_constraint(v, pltpu.HBM) for v in (features, cotangent, weight.reshape(3, STACK, FULL))))
    return grad_input, grad_weight[:27].astype(F32)


def solution(mesh):
    placed = (P("sp", "ch", None), P(None, "ch", None), P("sp", "ch", None))
    return jax.shard_map(
        local,
        mesh=mesh,
        in_specs=placed,
        out_specs=(P("sp", "ch", None), P(None, "ch", None)),
        check_vma=False,
    )
```
